128 devices in a mesh: net: 32 (over x, y, core), dev: 4 (over z).
Axes of the slice: x: 4, y: 4, z: 4, core: 2. Of those that a mesh axis runs over, the one named last changes fastest.
Arguments:
- zinv: float32 [128, 1024, 1024], P('net', 'dev')
- source: float32 [131072], P('net'), may hold values from -4 to 4
- model_state: float32 [16384, 128], P(('net', 'dev')), may hold values from -6 to 6
- propagator: float32 [16384, 128, 128], P(('net', 'dev')), may hold values from -0.4375 to 0.4375
- input_gain: float32 [16384, 128], P(('net', 'dev')), may hold values from -3 to 3
- output_gain: float32 [16384, 128], P(('net', 'dev')), may hold values from -0.5 to 0.5
- model_owner: int32 [16384, 1], P(('net', 'dev')), may hold values from 0 to 31; in each aligned block of 128 rows (0 to 127, 128 to 255, ...) at most 16 rows name the same one
- model_bus: int32 [16384], P(('net', 'dev')), may hold values from 0 to 4095
- line_from: int32 [16384], P('net'), may hold values from 0 to 4095
- line_to: int32 [16384], P('net'), may hold values from 0 to 4095
- line_delay: int32 [16384], P('net'), may hold values from 2 to 6
- line_imped: float32 [16384], P('net'), may hold values from 2 to 8
- wave_from_past: float32 [6, 16384], P(None, 'net'), may hold values from -6 to 6
- wave_to_past: float32 [6, 16384], P(None, 'net'), may hold values from -6 to 6
Outputs:
- voltage_trace: float32 [8, 131072], P(None, 'net')
- final_state: float32 [16384, 128], P(('net', 'dev'))
The draws below stay inside these ranges and needn't reach their ends.
Inputs may be any that keep to these rules, and one draw needn't show every extreme that they name: `model_owner`: among the models of one device (aligned blocks of 128 rows) at most 16 name the same owner, a bound that some block reaches.
All inputs are finite; a program needn't handle non-finite values.
Results may differ from the reference program's by a relative error of at most 0.0003.
Values sent between devices are 32-bit elements; how exact they have to be, the bound alone decides.
A program may use at most 128 MiB of HBM per device.

```python
import math
import jax
import jax.numpy as jnp
import numpy as np
from jax import lax

NB = 1024
STATE = 128
SUBS_DEV = 4
MODELS_DEV = 128
LINES_DEV = 512
STEPS = 8
DMIN = 2
DMAX = 6
BUS_DEV = 4096
BUSES = 131072
SUBNETS = 128
MODELS = 16384
CAP = 16
LINES = 16384
N_NET = 32


def draw_zinv(key, part):
    key = jax.random.fold_in(key, 11)
    diag_key, off_key = jax.random.split(key, 2)
    diagonal = jax.random.uniform(diag_key, (SUBNETS, NB), jnp.float32, 0.5, 1.0)
    off = 0.02 * jax.random.normal(off_key, (SUBNETS, NB, NB), jnp.float32)
    rows = jnp.arange(NB)[:, None]
    cols = jnp.arange(NB)[None, :]
    unit = (rows == cols).astype(jnp.float32)[None, :, :]
    return off * (1.0 - unit) + unit * diagonal[:, :, None]


def place_ends(drawn, key, low, top_value):
    extent = drawn.shape
    spot = [jax.random.randint(jax.random.fold_in(key, axis), (), 0, extent[axis]) for axis in range(len(extent))]
    drawn = drawn.at[tuple(spot)].set(low)
    longest = extent.index(max(extent))
    spot[longest] = (spot[longest] + 1) % extent[longest]
    return drawn.at[tuple(spot)].set(top_value)


def level_of(key, shape, cuts, smallest, high):
    def one(position, parts):
        steps = jax.random.uniform(jax.random.fold_in(jax.random.fold_in(key, 6), position), (parts,), jnp.float32, smallest / len(cuts), high / len(cuts))
        return jnp.repeat(jnp.exp(steps), shape[position] // parts).reshape((-1,) + (1,) * (len(shape) - position - 1))

    loudness = one(*cuts[0])
    for cut in cuts[1:]:
        loudness = loudness * one(*cut)
    return loudness


def assign_block(rng, own, number, rows, count, top, limit, lean):
    order = jax.random.permutation(rng, count)
    heavy_load, ordinary = shares(count, rows * top, limit, lean, True), shares(count, rows * top, limit, lean, False)
    places = jnp.arange(count)

    def named(tallies, rotation):
        used = int((tallies > 0).sum())
        fixed = max(1, used // 4)
        passed = fixed + (places - fixed + rotation * (used - fixed)) % max(1, count - fixed)
        return jnp.zeros((count,), jnp.int32).at[order[jnp.where(places < fixed, places, passed)]].set(jnp.asarray(tallies, jnp.int32))

    tallies = jnp.where(number % 4 == 0, named(heavy_load, number // 4), named(ordinary, number - number // 4 - 1))
    mixed = jax.random.permutation(jax.random.fold_in(own, 3), count)
    source_of, receiver = mixed[0:count // 2 * 2:2], mixed[1:count // 2 * 2:2]
    slack = jnp.minimum(tallies[source_of] - 1, limit - tallies[receiver]) // 2
    slack = jnp.where((source_of == order[0]) | (receiver == order[0]) | (tallies[receiver] == 0), 0, jnp.maximum(slack, 0))
    passed = jax.random.randint(jax.random.fold_in(own, 4), (count // 2,), 0, 1 << 20) % (slack + 1)
    tallies = tallies.at[source_of].add(-passed).at[receiver].add(passed)
    members = jnp.searchsorted(jnp.cumsum(tallies), jnp.arange(rows * top), side="right").astype(jnp.int32)
    table = members.reshape(top, rows).T
    table = table[jax.random.permutation(jax.random.fold_in(own, 1), rows)]
    rotation = jax.random.randint(jax.random.fold_in(own, 2), (rows, 1), 0, top)
    return jnp.take_along_axis(table, (jnp.arange(top)[None, :] + rotation) % top, axis=1)


def shares(amount, total, limit, skew, full):
    portions = [(1 << 20) // math.isqrt(standing ** skew) + 1 for standing in range(1, amount + 1)]
    largest = limit if full else min(limit, max(-(-total // amount), total * portions[0] // sum(portions)))
    least = 1 if total - largest >= amount - 1 else 0
    given, surplus = [largest] + [least] * (amount - 1), total - largest - least * (amount - 1)
    while surplus > 0:
        movable = [i for i in range(1, amount) if given[i] < largest] or [i for i in range(1, amount) if given[i] < limit]
        mass, remaining = sum([portions[i] for i in movable]), surplus
        for i in movable:
            addition = min(limit - given[i], max(1, remaining * portions[i] // mass), surplus)
            given[i] = given[i] + addition
            surplus = surplus - addition
    return np.array(given)


def scatter_about(key, dims, spread, most, pieces=(), dtype=jnp.bfloat16):
    drawn = spread * jax.random.normal(key, dims, jnp.float32)
    if pieces:
        drawn = drawn * level_of(key, dims, pieces, -0.22, 0.18)
    return jnp.clip(drawn, -most, most).astype(dtype)


def setup_inputs(seed: int = 0) -> dict:
    seeds = jax.random.split(jax.random.key(seed), 15)
    zinv = draw_zinv(jax.random.fold_in(seeds[14], 71), 0)
    source = scatter_about(seeds[1], (BUSES,), 0.5, 4.0, ((0, 32),), jnp.float32)
    model_state = scatter_about(seeds[2], (MODELS, STATE), 1.0, 6.0, ((0, 128),), jnp.float32)
    propagator = scatter_about(seeds[3], (MODELS, STATE, STATE), (3 * STATE // 2) ** -0.5, 0.4375, ((0, 128),), jnp.float32)
    input_gain = scatter_about(seeds[4], (MODELS, STATE), 0.5, 3.0, ((0, 128),), jnp.float32)
    output_gain = scatter_about(seeds[5], (MODELS, STATE), STATE ** -0.5, 0.5, ((0, 128),), jnp.float32)
    model_owner_keys = jax.random.split(jax.random.fold_in(seeds[6], 1), MODELS // MODELS_DEV)
    model_owner_turns = jax.random.permutation(jax.random.fold_in(seeds[6], 3), MODELS // MODELS_DEV)
    model_owner = jax.vmap(lambda own, number: assign_block(jax.random.fold_in(seeds[6], 2), own, number, MODELS_DEV, N_NET, 1, CAP, 2))(model_owner_keys, model_owner_turns).reshape((MODELS, 1))
    model_bus = place_ends(jax.random.randint(seeds[7], (MODELS,), 0, BUS_DEV), jax.random.fold_in(seeds[7], 1), 0, BUS_DEV - 1).astype(jnp.int32)
    line_from = place_ends(jax.random.randint(seeds[8], (LINES,), 0, BUS_DEV), jax.random.fold_in(seeds[8], 1), 0, BUS_DEV - 1).astype(jnp.int32)
    line_to = place_ends(jax.random.randint(seeds[9], (LINES,), 0, BUS_DEV), jax.random.fold_in(seeds[9], 1), 0, BUS_DEV - 1).astype(jnp.int32)
    line_delay = place_ends(jax.random.randint(seeds[10], (LINES,), DMIN, DMAX + 1), jax.random.fold_in(seeds[10], 1), DMIN, DMAX).astype(jnp.int32)
    line_imped = jnp.clip(jnp.exp(math.log(8.0) - 1.3862944 * jax.random.uniform(seeds[11], (LINES,), jnp.float32) ** level_of(seeds[11], (LINES,), ((0, 32),), -0.2, 0.2)), 2.0, 8.0)
    wave_from_past = scatter_about(seeds[12], (DMAX, LINES), 1.0, 6.0, ((1, 32),), jnp.float32)
    wave_to_past = scatter_about(seeds[13], (DMAX, LINES), 1.0, 6.0, ((1, 32),), jnp.float32)
    return {"zinv": zinv, "source": source, "model_state": model_state, "propagator": propagator, "input_gain": input_gain, "output_gain": output_gain, "model_owner": model_owner, "model_bus": model_bus, "line_from": line_from, "line_to": line_to, "line_delay": line_delay, "line_imped": line_imped, "wave_from_past": wave_from_past, "wave_to_past": wave_to_past}


def reference(zinv, source, model_state, propagator, input_gain, output_gain, model_owner, model_bus, line_from, line_to, line_delay, line_imped, wave_from_past, wave_to_past):
    bus_count = SUBS_DEV * NB * N_NET
    model_index = (model_owner[:, 0] * (SUBS_DEV * NB) + model_bus).astype(jnp.int32)
    line_net = (jnp.arange(LINES) // LINES_DEV).astype(jnp.int32)
    from_index = (line_net * (SUBS_DEV * NB) + line_from).astype(jnp.int32)
    to_index = (((line_net + 1) % N_NET) * (SUBS_DEV * NB) + line_to).astype(jnp.int32)
    from_waves = jnp.zeros((DMAX + STEPS, LINES), jnp.float32).at[:DMAX].set(wave_from_past)
    to_waves = jnp.zeros((DMAX + STEPS, LINES), jnp.float32).at[:DMAX].set(wave_to_past)
    state = model_state
    traces = []
    for moment in range(STEPS):
        lookback = (moment + DMAX - line_delay).astype(jnp.int32)
        arrive_from = jnp.take_along_axis(to_waves, lookback[None, :], 0)[0]
        arrive_to = jnp.take_along_axis(from_waves, lookback[None, :], 0)[0]
        currents = jnp.sum(state * output_gain, 1)
        model_inj = jnp.zeros((bus_count,), jnp.float32).at[model_index].add(currents)
        line_inj = jnp.zeros((bus_count,), jnp.float32).at[from_index].add(arrive_from).at[to_index].add(arrive_to)
        injection = source + model_inj + line_inj
        volts = jnp.einsum("sij,sj->si", zinv, injection.reshape(SUBNETS, NB), precision=lax.Precision.HIGHEST).reshape(bus_count)
        from_waves = from_waves.at[DMAX + moment].set(2.0 * volts[from_index] / line_imped - arrive_from)
        to_waves = to_waves.at[DMAX + moment].set(2.0 * volts[to_index] / line_imped - arrive_to)
        model_volts = volts[model_index]
        state = jnp.einsum("ms,mst->mt", state, propagator, precision=lax.Precision.HIGHEST) + model_volts[:, None] * input_gain
        traces.append(volts)
    return jnp.stack(traces), state
```

```python
import functools
import jax
import jax.numpy as jnp
from jax import lax
from jax.experimental import pallas as pl
from jax.experimental.pallas import tpu as pltpu
from jax.sharding import PartitionSpec as P

STEPS = 8
DMIN = 2
DMAX = 6
NETS = 32
DEVS = 4
CAP = 16
F32 = jnp.float32
BF16 = jnp.bfloat16
MESH = pl.DeviceIdType.MESH


def rows_sum(x):
    return jnp.sum(x, axis=0, keepdims=True)


def parts(x, count=3):
    pieces = []
    for i in range(count):
        piece = x.astype(BF16)
        pieces.append(piece)
        if i + 1 < count:
            x = x - piece.astype(F32)
    return pieces


def dot(a, b, dims):
    return lax.dot_general(a, b, (dims, ((), ())), preferred_element_type=F32)


def nn(a, b):
    return dot(a, b, ((1,), (0,)))


def nt(a, b):
    return dot(a, b, ((1,), (1,)))


def tn(a, b):
    return dot(a, b, ((0,), (0,)))


def iota(shape, dim):
    return lax.broadcasted_iota(jnp.int32, shape, dim)


def iota_f(shape, dim):
    return iota(shape, dim).astype(F32)


def one(mask):
    return jnp.where(mask, 1.0, 0.0).astype(F32)


def third_sum(x):
    rows = x.shape[0] // 3
    return x[:rows] + x[rows:2 * rows] + x[2 * rows:]


def grid_kernel(z, src, lines, mod, fh, xb, trace, final,
                asend, arecv, vall, uv, prev, wsend, wrecv, rsend, rrecv, ohl, ohs,
                a_s, a_r, v_s, v_r, uv_s, uv_r, w_s, w_r, l_s, l_r, r_s, r_r):
    n = lax.axis_index("net")
    d = lax.axis_index("dev")

    def net(k):
        return lax.rem(n + k, NETS)

    def dev(j):
        return lax.rem(d + j, DEVS)

    def copy(a, b, send, recv, to_net, to_dev):
        return pltpu.make_async_remote_copy(src_ref=a, dst_ref=b, send_sem=send, recv_sem=recv,
                                            device_id=(to_net, to_dev), device_id_type=MESH)

    bar = pltpu.get_barrier_semaphore()

    def greet(to_net, to_dev):
        pl.semaphore_signal(bar, inc=1, device_id=(to_net, to_dev), device_id_type=MESH)

    lax.fori_loop(1, NETS, lambda k, _: (greet(net(k), d), 0)[1], 0)
    for j in range(1, DEVS):
        greet(n, dev(j))
        greet(net(1), dev(j))
        greet(net(NETS - 1), dev(j))
    pl.semaphore_wait(bar, NETS - 1 + 3 * (DEVS - 1))

    line_copy = copy(lines, prev, l_s, l_r, net(1), d)
    line_copy.start()

    owner = mod[0:1, :]
    offset = owner - n.astype(F32)
    offset = jnp.where(offset < 0.0, offset + float(NETS), offset)
    wide = jnp.broadcast_to(owner, (128, 128))
    earlier = one(wide.T == wide) * one(iota((128, 128), 0) < iota((128, 128), 1))
    rank = rows_sum(earlier)
    own = one(iota_f((NETS, 128), 0) == offset)
    own_b = own.astype(BF16)
    seat = one(iota_f((CAP, 128), 0) == rank)
    values = [fh[q:q + 1, :] for q in range(15)] + [mod[1:2, :] + 1.0]
    table = jnp.concatenate([value * seat for value in values], axis=0)
    packed = sum(nt(own_b, piece) for piece in parts(table))
    asend[:, 0, :] = packed
    arecv[0] = packed[0:1, :]

    def a_copy(k):
        return copy(asend.at[k], arecv.at[k], a_s.at[k], a_r.at[k], net(k), d)

    lax.fori_loop(1, NETS, lambda k, _: (a_copy(k).start(), 0)[1], 0)

    line_copy.wait_recv()
    ends = jnp.concatenate([lines[9:10, :], prev[0:1, :]], axis=1)
    delay = jnp.concatenate([lines[1:2, :], prev[1:2, :]], axis=1)
    twice = 2.0 / jnp.concatenate([lines[2:3, :], prev[2:3, :]], axis=1)
    waves = [jnp.concatenate([lines[10 + i:11 + i, :], prev[3 + i:4 + i, :]], axis=1) for i in range(DMAX)]
    high = jnp.floor(ends * (1.0 / 128.0))
    low = ends - 128.0 * high
    row = iota((8, 1), 0)
    row_high = ((row // 2) * 8 + 2 * d + row % 2).astype(F32)
    end_row = one(high == row_high)
    mine = rows_sum(end_row)
    ohl[...] = one(iota_f((128, 1024), 0) == low).astype(BF16)

    def arrivals(t):
        got = jnp.zeros((1, 1024), F32)
        for lag in range(DMIN, DMAX + 1):
            if DMAX + t - lag < len(waves):
                got = jnp.where(delay == float(lag), waves[DMAX + t - lag], got)
        return got

    def inject(arrive):
        pieces = jnp.concatenate(parts(end_row * arrive), axis=0)
        return third_sum(nt(pieces, ohl[...]))

    def sample(volts):
        pieces = jnp.concatenate(parts(volts), axis=0)
        return rows_sum(third_sum(nn(pieces, ohl[...])) * end_row)

    arrive = [arrivals(0), arrivals(1)]
    line_part = [inject(arrive[0]), inject(arrive[1])]

    seat_mask = one(iota((CAP, 256), 1) % CAP == iota((CAP, 256), 0))
    lax.fori_loop(1, NETS, lambda k, _: (a_copy(k).wait_recv(), 0)[1], 0)
    spread = jnp.concatenate([arecv[k] * seat_mask for k in range(NETS)], axis=0)
    collect = one(iota((16, 256), 1) // CAP == iota((16, 256), 0)).astype(BF16)
    vall[d] = sum(nt(collect, piece) for piece in parts(spread))

    def v_copy(j):
        return copy(vall.at[d], vall.at[d], v_s.at[j], v_r.at[d], n, dev(j))

    def v_wait(j):
        return copy(vall.at[dev(j)], vall.at[dev(j)], v_s.at[j], v_r.at[dev(j)], n, dev(j))

    for j in range(1, DEVS):
        v_copy(j).start()
    total = jnp.zeros((360, 128), F32)
    slot_high = None
    for j in range(DEVS):
        if j:
            v_wait(j).wait_recv()
        vals = vall[dev(j)]
        bus = vals[15:16, :] - 1.0
        b_high = jnp.floor(bus * (1.0 / 128.0))
        b_low = bus - 128.0 * b_high
        hot = one(iota_f((128, 512), 0) == b_low).astype(BF16)
        if j == 0:
            slot_high = b_high
            ohs[...] = hot
        b_row = one(b_high == row_high)
        left = jnp.concatenate([vals[q:q + 1, :] * b_row for q in range(15)], axis=0)
        total = total + nt(jnp.concatenate(parts(left), axis=0), hot)
    total = third_sum(total)
    free = [total[8 * q:8 * q + 8] for q in range(8)]
    gain = [total[8 * q:8 * q + 8] for q in range(8, 15)]
    source = jnp.concatenate([src[s, d] for s in range(4)], axis=0)

    def uv_copy(t, j):
        return copy(uv.at[t, d], uv.at[t, d], uv_s.at[t, j], uv_r.at[t, d], n, dev(j))

    def uv_wait(t, j):
        return copy(uv.at[t, dev(j)], uv.at[t, dev(j)], uv_s.at[t, j], uv_r.at[t, dev(j)], n, dev(j))

    def w_copy(t, way, j):
        return copy(wsend.at[t, way], wrecv.at[t, way, d], w_s.at[t, way, j], w_r.at[t, way, d],
                    net(1 if way == 0 else NETS - 1), dev(j))

    def w_wait(t, way, j):
        return copy(wsend.at[t, way], wrecv.at[t, way, dev(j)], w_s.at[t, way, j], w_r.at[t, way, dev(j)],
                    net(1 if way == 0 else NETS - 1), dev(j))

    def solve(t):
        rows = []
        for s in range(4):
            total = None
            for c in range(8):
                term = z[s, :, 128 * c:128 * c + 128] * uv[t, c // 2, 0, 2 * s + c % 2:2 * s + c % 2 + 1, :]
                total = term if total is None else total + term
            rows.append(rows_sum(total[:128].T))
            rows.append(rows_sum(total[128:].T))
        return jnp.concatenate(rows, axis=0)

    def keep(t):
        for c in range(8):
            for s in range(4):
                at = 1024 * s + 128 * c
                trace[t:t + 1, at:at + 128] = uv[t + 1, c // 2, 1, 2 * s + c % 2:2 * s + c % 2 + 1, :]

    uv[0, d, 0] = source + free[0] + line_part[0]
    uv[0, d, 1] = jnp.zeros((8, 128), F32)
    for j in range(1, DEVS):
        uv_copy(0, j).start()
    volts = []
    for t in range(STEPS):
        for j in range(1, DEVS):
            uv_wait(t, j).wait_recv()
        v = solve(t)
        volts.append(v)
        if t + 1 < STEPS:
            if t >= 1:
                for way in range(2):
                    for j in range(DEVS):
                        w_wait(t - 1, way, j).wait_recv()
                waves.append(jnp.concatenate([sum(wrecv[t - 1, 1, j] for j in range(DEVS)),
                                              sum(wrecv[t - 1, 0, j] for j in range(DEVS))], axis=1))
                arrive.append(arrivals(t + 1))
                line_part.append(inject(arrive[t + 1]))
            u = source + free[t + 1] + line_part[t + 1]
            for k in range(t + 1):
                u = u + gain[t - k] * volts[k]
        else:
            u = jnp.zeros((8, 128), F32)
        uv[t + 1, d, 0] = u
        uv[t + 1, d, 1] = v
        for j in range(1, DEVS):
            uv_copy(t + 1, j).start()
        if t <= STEPS - 1 - DMIN:
            wave = mine * (sample(v) * twice - arrive[t])
            wsend[t, 0] = wave[:, :512]
            wsend[t, 1] = wave[:, 512:]
            for way in range(2):
                for j in range(DEVS):
                    w_copy(t, way, j).start()
        if t:
            keep(t - 1)
    for j in range(1, DEVS):
        uv_wait(STEPS, j).wait_recv()

    full = jnp.concatenate([uv[t + 1, c, 1] for t in range(STEPS) for c in range(DEVS)], axis=0)
    reached = sum(nn(piece, ohs[...]) for piece in parts(full))
    row32 = iota((32, 1), 0)
    high32 = (((row32 % 8) // 2) * 8 + 2 * (row32 // 8) + row32 % 2).astype(F32)
    pick = one(slot_high == high32)
    at_slot = [rows_sum(reached[32 * t:32 * t + 32] * pick) for t in range(STEPS)]
    seat512 = one(iota((CAP, 512), 1) % CAP == iota((CAP, 512), 0))
    home = one(iota((NETS, 512), 1) // CAP == iota((NETS, 512), 0)).astype(BF16)
    table = jnp.concatenate([x * seat512 for x in at_slot], axis=0)
    back = sum(nt(home, piece) for piece in parts(table))
    rsend[:, 0, :] = back
    rrecv[0] = back[0:1, :]

    def r_copy(k):
        return copy(rsend.at[k], rrecv.at[k], r_s.at[k], r_r.at[k], net(NETS - k), d)

    lax.fori_loop(1, NETS, lambda k, _: (r_copy(k).start(), 0)[1], 0)
    keep(STEPS - 1)

    def drain(k, _):
        a_copy(k).wait_send()
        r_copy(k).wait_send()
        r_copy(k).wait_recv()
        return 0

    lax.fori_loop(1, NETS, drain, 0)
    answer = rrecv[:, 0, :]
    at_model = sum(tn(piece, own_b) for piece in parts(answer))
    state = xb[0]
    for t in range(STEPS):
        mv = rows_sum(at_model[CAP * t:CAP * t + CAP] * seat)
        state = state + mv * xb[STEPS - t]
    final[...] = state.T

    line_copy.wait_send()
    for j in range(1, DEVS):
        v_copy(j).wait_send()
        for t in range(STEPS + 1):
            uv_copy(t, j).wait_send()
    for t in range(STEPS - DMIN):
        for way in range(2):
            for j in range(DEVS):
                w_copy(t, way, j).wait_send()


def model_kernel(prop, state, bgain, og, fh, xb, raw, at, xs, bs, sems, *, unroll):
    def cp(c):
        return pltpu.make_async_copy(prop.at[:, pl.ds(8 * c, 8), :], raw.at[c], sems.at[c])
    for c in range(16):
        cp(c).start()
    xs[...] = state[...].T
    bs[...] = bgain[...].T
    ogt = og[...].T
    fh[0:1, :] = rows_sum(xs[...] * ogt)
    fh[8:9, :] = rows_sum(bs[...] * ogt)
    fh[15:16, :] = jnp.zeros((1, 128), F32)
    xb[1] = bs[...]
    flat = raw.reshape(16, 1024, 128)

    def first(c, acc):
        cp(c).wait()
        ax, ab = acc
        for kk in range(8):
            a = flat[c, pl.ds(kk, 128, stride=8), :].T
            k = 8 * c + kk
            at[k] = a
            ax = ax + a * xs[pl.ds(k, 1), :]
            ab = ab + a * bs[pl.ds(k, 1), :]
        return ax, ab

    zero = jnp.zeros((128, 128), F32)
    ax, ab = lax.fori_loop(0, 16, first, (zero, zero))

    def later(i, acc):
        ax, ab = acc
        for kk in range(unroll):
            k = i * unroll + kk
            a = at[k]
            ax = ax + a * xs[pl.ds(k, 1), :]
            ab = ab + a * bs[pl.ds(k, 1), :]
        return ax, ab

    for it in range(1, 9):
        xs[...] = ax
        bs[...] = ab
        if it < 8:
            fh[it:it + 1, :] = rows_sum(ax * ogt)
            if it < 7:
                fh[8 + it:9 + it, :] = rows_sum(ab * ogt)
            xb[1 + it] = ab
            ax, ab = lax.fori_loop(0, 128 // unroll, later, (zero, zero))
        else:
            xb[0] = ax

def models(prop, state, bgain, og, unroll=4):
    v = pl.BlockSpec(memory_space=pltpu.VMEM)
    return pl.pallas_call(
        functools.partial(model_kernel, unroll=unroll),
        out_shape=(jax.ShapeDtypeStruct((16, 128), F32), jax.ShapeDtypeStruct((9, 128, 128), F32)),
        in_specs=[pl.BlockSpec(memory_space=pl.ANY), v, v, v],
        out_specs=(v, v),
        scratch_shapes=[pltpu.VMEM((16, 128, 8, 128), F32), pltpu.VMEM((128, 128, 128), F32),
                        pltpu.VMEM((128, 128), F32), pltpu.VMEM((128, 128), F32), pltpu.SemaphoreType.DMA((16,))],
        compiler_params=pltpu.CompilerParams(vmem_limit_bytes=40 << 20),
    )(prop, state, bgain, og)


def steps_call(z, src, lines, mod, fh, xb):
    v = pl.BlockSpec(memory_space=pltpu.VMEM)
    dma = pltpu.SemaphoreType.DMA
    return pl.pallas_call(
        grid_kernel,
        out_shape=(jax.ShapeDtypeStruct((STEPS, 4096), F32), jax.ShapeDtypeStruct((128, 128), F32)),
        in_specs=[v] * 6,
        out_specs=(v, v),
        scratch_shapes=[
            pltpu.VMEM((NETS, 1, 256), F32), pltpu.VMEM((NETS, 1, 256), F32),
            pltpu.VMEM((DEVS, 16, 512), F32), pltpu.VMEM((STEPS + 1, DEVS, 2, 8, 128), F32),
            pltpu.VMEM((16, 512), F32), pltpu.VMEM((6, 2, 1, 512), F32), pltpu.VMEM((6, 2, DEVS, 1, 512), F32),
            pltpu.VMEM((NETS, 1, 128), F32), pltpu.VMEM((NETS, 1, 128), F32),
            pltpu.VMEM((128, 1024), BF16), pltpu.VMEM((128, 512), BF16),
            dma((NETS,)), dma((NETS,)), dma((DEVS,)), dma((DEVS,)), dma((STEPS + 1, DEVS)), dma((STEPS + 1, DEVS)),
            dma((6, 2, DEVS)), dma((6, 2, DEVS)), dma, dma, dma((NETS,)), dma((NETS,)),
        ],
        compiler_params=pltpu.CompilerParams(collective_id=0, has_side_effects=True, vmem_limit_bytes=40 << 20),
    )(z, src, lines, mod, fh, xb)


def body(zinv, source, model_state, propagator, input_gain, output_gain, model_owner, model_bus,
         line_from, line_to, line_delay, line_imped, wave_from_past, wave_to_past):
    def r(x):
        return x.astype(F32)[None, :]
    lines = jnp.concatenate([r(line_to), r(line_delay), r(line_imped), wave_from_past, r(line_from), wave_to_past], axis=0)
    mod = jnp.concatenate([r(model_owner[:, 0]), r(model_bus), jnp.zeros((6, 128), F32)], axis=0)
    fh, xb = models(propagator, model_state, input_gain, output_gain)
    return steps_call(zinv, source.reshape(4, 4, 2, 128), lines, mod, fh, xb)


def solution(mesh):
    one_axis, both = P("net"), P(("net", "dev"))
    two = P(("net", "dev"), None)
    in_specs = (P("net", "dev", None), one_axis, two, P(("net", "dev"), None, None), two, two, two, both,
                one_axis, one_axis, one_axis, one_axis, P(None, "net"), P(None, "net"))
    return jax.shard_map(body, mesh=mesh, in_specs=in_specs, out_specs=(P(None, "net"), two), check_vma=False)
```

```python
import jax
import jax.numpy as jnp
from jax import lax
from jax.experimental import pallas as pl
from jax.experimental.pallas import tpu as pltpu
from jax.sharding import PartitionSpec as P

STEPS = 8
DMIN = 2
DMAX = 6
NETS = 32
DEVS = 4
CAP = 16
F32 = jnp.float32
BF16 = jnp.bfloat16
MESH = pl.DeviceIdType.MESH


def rows_sum(x):
    return jnp.sum(x, axis=0, keepdims=True)


def parts(x, count=3):
    pieces = []
    for i in range(count):
        piece = x.astype(BF16)
        pieces.append(piece)
        if i + 1 < count:
            x = x - piece.astype(F32)
    return pieces


def dot(a, b, dims):
    return lax.dot_general(a, b, (dims, ((), ())), preferred_element_type=F32)


def nn(a, b):
    return dot(a, b, ((1,), (0,)))


def nt(a, b):
    return dot(a, b, ((1,), (1,)))


def tn(a, b):
    return dot(a, b, ((0,), (0,)))


def iota(shape, dim):
    return lax.broadcasted_iota(jnp.int32, shape, dim)


def iota_f(shape, dim):
    return iota(shape, dim).astype(F32)


def one(mask):
    return jnp.where(mask, 1.0, 0.0).astype(F32)


def third_sum(x):
    rows = x.shape[0] // 3
    return x[:rows] + x[rows:2 * rows] + x[2 * rows:]


def grid_kernel(zinv, source, state0, prop, bgain, ogain, owner_i, bus_i, from_i, to_i, delay_i, imped_i, fpast, tpast,
                trace, final,
                z, src, st, gi, go, own_v, bus_v, from_v, to_v, delay_v, imped_v, fp, tp,
                raw, at, xs, bs, xb, asend, arecv, vall, uv, pack, prev, wsend, wrecv, rsend, rrecv,
                ohl, hots, brow, acc, jl,
                in_s, raw_s, a_s, a_r, v_s, v_r, uv_s, uv_r, w_s, w_r, l_s, l_r, r_s, r_r):
    n = lax.axis_index("net")
    d = lax.axis_index("dev")

    def net(k):
        return lax.rem(n + k, NETS)

    def dev(j):
        return lax.rem(d + j, DEVS)

    def copy(a, b, send, recv, to_net, to_dev):
        return pltpu.make_async_remote_copy(src_ref=a, dst_ref=b, send_sem=send, recv_sem=recv,
                                            device_id=(to_net, to_dev), device_id_type=MESH)

    def others(run):
        lax.fori_loop(1, NETS, lambda k, _: (run(k), 0)[1], 0)

    pairs = [(state0, st), (bgain, gi), (ogain, go), (owner_i, own_v), (bus_i, bus_v), (from_i, from_v), (to_i, to_v),
             (delay_i, delay_v), (imped_i, imped_v), (fpast, fp), (tpast, tp), (source, src), (zinv, z)]
    loads = [pltpu.make_async_copy(a, b, in_s.at[i]) for i, (a, b) in enumerate(pairs)]

    def raw_copy(c):
        return pltpu.make_async_copy(prop.at[:, pl.ds(8 * c, 8), :], raw.at[c], raw_s.at[c])

    for load in loads[:11]:
        load.start()
    for c in range(16):
        raw_copy(c).start()
    for load in loads[11:]:
        load.start()

    bar = pltpu.get_barrier_semaphore()

    def greet(to_net, to_dev):
        pl.semaphore_signal(bar, inc=1, device_id=(to_net, to_dev), device_id_type=MESH)

    others(lambda k: greet(net(k), d))
    for j in range(1, DEVS):
        greet(n, dev(j))
        greet(net(1), dev(j))
        greet(net(NETS - 1), dev(j))

    for load in loads[:11]:
        load.wait()
    owner = own_v[...].astype(F32)
    offset = owner - n.astype(F32)
    offset = jnp.where(offset < 0.0, offset + float(NETS), offset)
    wide = jnp.broadcast_to(owner, (128, 128))
    earlier = one(wide.T == wide) * one(iota((128, 128), 0) < iota((128, 128), 1))
    rank = rows_sum(earlier)
    own = one(iota_f((NETS, 128), 0) == offset).astype(BF16)
    seat = one(iota_f((CAP, 128), 0) == rank)
    ogt = go[...].T
    go[...] = ogt
    first_x = st[...].T
    first_b = gi[...].T
    xs[...] = first_x
    bs[...] = first_b
    xb[0] = first_b
    free_m = [rows_sum(first_x * ogt)]
    gain_m = [rows_sum(first_b * ogt)]
    pack[0:1, :] = to_v[...].astype(F32)
    pack[1:2, :] = delay_v[...].astype(F32)
    pack[2:3, :] = imped_v[...]
    pack[3:9, :] = fp[...]
    pack[9:16, :] = jnp.zeros((7, 512), F32)

    flat = raw.reshape(16, 1024, 128)
    zero = jnp.zeros((128, 128), F32)

    def first(c, held):
        raw_copy(c).wait()
        ax, ab = held
        for kk in range(8):
            k = 8 * c + kk
            a = flat[c, pl.ds(kk, 128, stride=8), :].T
            at[k] = a
            ax = ax + a * xs[pl.ds(k, 1), :]
            ab = ab + a * bs[pl.ds(k, 1), :]
        return ax, ab

    def later(i, held):
        ax, ab = held
        for kk in range(8):
            k = 8 * i + kk
            a = at[k]
            ax = ax + a * xs[pl.ds(k, 1), :]
            ab = ab + a * bs[pl.ds(k, 1), :]
        return ax, ab

    def product(step):
        ax, ab = lax.fori_loop(0, 16, later if step else first, (zero, zero))
        xs[...] = ax
        if step + 1 < STEPS:
            bs[...] = ab
            xb[step + 1] = ab
            free_m.append(rows_sum(ax * go[...]))
            gain_m.append(rows_sum(ab * go[...]))

    def a_copy(b, k):
        return copy(asend.at[b, k], arecv.at[b, k], a_s.at[b, k], a_r.at[b, k], net(k), d)

    def send_batch(b, values):
        table = [value * seat for value in values]
        table.append(jnp.zeros((128 - CAP * len(values), 128), F32))
        packed = sum(nt(own, piece) for piece in parts(jnp.concatenate(table, axis=0)))
        asend[b, :, 0, :] = packed
        arecv[b, 0] = packed[0:1, :]
        others(lambda k: a_copy(b, k).start())

    def v_copy(b, j):
        return copy(vall.at[b, d], vall.at[b, d], v_s.at[b, j], v_r.at[b, d], n, dev(j))

    def v_wait(b, j):
        return copy(vall.at[b, dev(j)], vall.at[b, dev(j)], v_s.at[b, j], v_r.at[b, dev(j)], n, dev(j))

    def share_batch(b):
        others(lambda k: a_copy(b, k).wait_recv())
        mask = one(iota((CAP, 128), 1) % CAP == iota((CAP, 128), 0))
        collect = one(iota((8, 128), 1) // CAP == iota((8, 128), 0)).astype(BF16)
        spread = jnp.concatenate([arecv[b, k] * mask for k in range(NETS)], axis=0)
        vall[b, d] = sum(nt(collect, piece) for piece in parts(spread))
        for j in range(1, DEVS):
            v_copy(b, j).start()

    row = iota((8, 1), 0)
    row_high = ((row // 2) * 8 + 2 * d + row % 2).astype(F32)
    row32 = iota((32, 1), 0)
    high32 = (((row32 % 8) // 2) * 8 + 2 * (row32 // 8) + row32 % 2).astype(F32)
    slot_high = []

    def place_batch(b, count):
        total = jnp.zeros((24 * count, 128), F32)
        for j in range(DEVS):
            if j:
                v_wait(b, j).wait_recv()
            vals = vall[b, dev(j)]
            if b == 0:
                bus = vals[3:4, :] - 1.0
                b_high = jnp.floor(bus * (1.0 / 128.0))
                slot_high.append(b_high)
                hots[j] = one(iota_f((128, 512), 0) == bus - 128.0 * b_high).astype(BF16)
                brow[j] = one(b_high == row_high)
            held = brow[j]
            left = jnp.concatenate([vals[q:q + 1, :] * held for q in range(count)], axis=0)
            total = total + nt(jnp.concatenate(parts(left), axis=0), hots[j])
        total = third_sum(total)
        return [total[8 * q:8 * q + 8] for q in range(count)]

    product(0)
    pl.semaphore_wait(bar, NETS - 1 + 3 * (DEVS - 1))
    line_copy = copy(pack, prev, l_s, l_r, net(1), d)
    line_copy.start()
    send_batch(0, [free_m[0], free_m[1], gain_m[0], bus_v[...].astype(F32) + 1.0])
    product(1)
    product(2)
    product(3)
    send_batch(1, free_m[2:5] + gain_m[1:4])

    line_copy.wait_recv()
    ends = jnp.concatenate([from_v[...].astype(F32), prev[0:1, :]], axis=1)
    delay = jnp.concatenate([pack[1:2, :], prev[1:2, :]], axis=1)
    twice = 2.0 / jnp.concatenate([pack[2:3, :], prev[2:3, :]], axis=1)
    waves = [jnp.concatenate([tp[i:i + 1, :], prev[3 + i:4 + i, :]], axis=1) for i in range(DMAX)]
    high = jnp.floor(ends * (1.0 / 128.0))
    ohl[...] = one(iota_f((128, 1024), 0) == ends - 128.0 * high).astype(BF16)
    mine = rows_sum(one(high == row_high))

    def arrivals(t):
        got = jnp.zeros((1, 1024), F32)
        for lag in range(DMIN, DMAX + 1):
            if DMAX + t - lag < len(waves):
                got = jnp.where(delay == float(lag), waves[DMAX + t - lag], got)
        return got

    def inject(t):
        left = jnp.concatenate(parts(one(high == high32) * arrive[t]), axis=0)
        jl[t] = third_sum(nt(left, ohl[...])).reshape(DEVS, 8, 128)

    def sample(v):
        left = jnp.concatenate(parts(v), axis=0)
        return rows_sum(third_sum(nn(left, ohl[...])) * one(high == row_high))

    arrive = [arrivals(0), arrivals(1)]
    inject(0)
    inject(1)

    def uv_copy(t, j):
        return copy(uv.at[t, d], uv.at[t, d], uv_s.at[t, j], uv_r.at[t, d], n, dev(j))

    def uv_wait(t, j):
        return copy(uv.at[t, dev(j)], uv.at[t, dev(j)], uv_s.at[t, j], uv_r.at[t, dev(j)], n, dev(j))

    def uv_send(t, u, v):
        uv[t, d, 0] = u
        uv[t, d, 1] = v
        for j in (2, 1, 3):
            uv_copy(t, j).start()

    def w_copy(t, way, j):
        return copy(wsend.at[t, way], wrecv.at[t, way, d], w_s.at[t, way, j], w_r.at[t, way, d],
                    net(1 if way == 0 else NETS - 1), dev(j))

    def w_wait(t, way, j):
        return copy(wsend.at[t, way], wrecv.at[t, way, dev(j)], w_s.at[t, way, j], w_r.at[t, way, dev(j)],
                    net(1 if way == 0 else NETS - 1), dev(j))

    def send_waves(t):
        wave = mine * (sample(volts[t]) * twice - arrive[t])
        wsend[t, 0] = wave[:, :512]
        wsend[t, 1] = wave[:, 512:]
        for j in (2, 1, 3, 0):
            for way in range(2):
                w_copy(t, way, j).start()

    def take_waves(t):
        for way in range(2):
            for j in range(DEVS):
                w_wait(t, way, j).wait_recv()
        waves.append(jnp.concatenate([sum(wrecv[t, 1, j] for j in range(DEVS)),
                                      sum(wrecv[t, 0, j] for j in range(DEVS))], axis=1))
        arrive.append(arrivals(t + DMIN))
        inject(t + DMIN)

    def columns(t, c, s):
        tiles = uv[t, c, 0] + jl[t, c]
        total = None
        for e in range(2):
            lanes = pl.ds(pl.multiple_of(256 * c + 128 * e, 128), 128)
            term = z[s, :, lanes] * tiles[2 * s + e:2 * s + e + 1, :]
            total = term if total is None else total + term
        return total

    def solve(t):
        uv_wait(t, 1).wait_recv()
        uv_wait(t, 3).wait_recv()
        for s in range(4):
            acc[s] = columns(t, d, s) + columns(t, dev(1), s) + columns(t, dev(3), s)
        uv_wait(t, 2).wait_recv()
        rows = []
        for s in range(4):
            total = acc[s] + columns(t, dev(2), s)
            rows.append(rows_sum(total[:128].T))
            rows.append(rows_sum(total[128:].T))
        return jnp.concatenate(rows, axis=0)

    def keep(t):
        for c in range(8):
            for s in range(4):
                spot = 1024 * s + 128 * c
                trace[t:t + 1, spot:spot + 128] = uv[t + 1, c // 2, 1, 2 * s + c % 2:2 * s + c % 2 + 1, :]

    def r_copy(b, k):
        return copy(rsend.at[b, k], rrecv.at[b, k], r_s.at[b, k], r_r.at[b, k], net(NETS - k), d)

    def send_back(b, steps):
        full = jnp.concatenate([uv[t + 1, c, 1] for t in steps for c in range(DEVS)], axis=0)
        reached = sum(nn(piece, hots[0]) for piece in parts(full))
        pick = one(slot_high[0] == high32)
        seats = one(iota((CAP, 512), 1) % CAP == iota((CAP, 512), 0))
        home = one(iota((NETS, 512), 1) // CAP == iota((NETS, 512), 0)).astype(BF16)
        table = [rows_sum(reached[32 * i:32 * i + 32] * pick) * seats for i in range(len(steps))]
        table.append(jnp.zeros((128 - CAP * len(steps), 512), F32))
        back = sum(nt(home, piece) for piece in parts(jnp.concatenate(table, axis=0)))
        rsend[b, :, 0, :] = back
        rrecv[b, 0] = back[0:1, :]
        others(lambda k: r_copy(b, k).start())

    def add_back(b, steps, state):
        others(lambda k: r_copy(b, k).wait_recv())
        answer = rrecv[b, :, 0, :]
        at_model = sum(tn(piece, own) for piece in parts(answer))
        for i, t in enumerate(steps):
            state = state + rows_sum(at_model[CAP * i:CAP * i + CAP] * seat) * xb[STEPS - 1 - t]
        return state

    share_batch(0)
    product(4)
    product(5)
    free, gain, volts = [], [], []
    got = place_batch(0, 3)
    free += got[:2]
    gain += got[2:]
    for load in loads[11:]:
        load.wait()
    base = jnp.concatenate([src[s, d] for s in range(4)], axis=0)
    uv_send(0, base + free[0], jnp.zeros((8, 128), F32))
    for t in range(STEPS):
        if t == 0:
            product(6)
            send_batch(2, free_m[5:8] + gain_m[4:7])
            share_batch(1)
        if 1 <= t <= STEPS - DMIN:
            send_waves(t - 1)
        if t == 1:
            got = place_batch(1, 6)
            free += got[:3]
            gain += got[3:]
        if t == 2:
            share_batch(2)
        if t >= 2:
            take_waves(t - 2)
            keep(t - 2)
        if t == 3:
            got = place_batch(2, 6)
            free += got[:3]
            gain += got[3:]
        if t == 4:
            product(7)
        ready = base
        if t + 1 < STEPS:
            ready = ready + free[t + 1]
            for k in range(t):
                ready = ready + gain[t - k] * volts[k]
        v = solve(t)
        volts.append(v)
        uv_send(t + 1, ready + gain[0] * v if t + 1 < STEPS else jnp.zeros((8, 128), F32), v)
    keep(STEPS - 2)
    send_back(0, list(range(STEPS - 1)))
    for j in range(1, DEVS):
        uv_wait(STEPS, j).wait_recv()
    send_back(1, [STEPS - 1])
    keep(STEPS - 1)

    def drain(k):
        for b in range(3):
            a_copy(b, k).wait_send()

    others(drain)
    line_copy.wait_send()
    for j in range(1, DEVS):
        for b in range(3):
            v_copy(b, j).wait_send()
        for t in range(STEPS + 1):
            uv_copy(t, j).wait_send()
    for t in range(STEPS - DMIN):
        for way in range(2):
            for j in range(DEVS):
                w_copy(t, way, j).wait_send()
    state = add_back(0, list(range(STEPS - 1)), xs[...])
    state = add_back(1, [STEPS - 1], state)
    final[...] = state.T

    def drain_back(k):
        for b in range(2):
            r_copy(b, k).wait_send()

    others(drain_back)


def body(zinv, source, model_state, propagator, input_gain, output_gain, model_owner, model_bus,
         line_from, line_to, line_delay, line_imped, wave_from_past, wave_to_past):
    vmem, dma = pltpu.VMEM, pltpu.SemaphoreType.DMA
    i32 = jnp.int32
    scratch = [
        vmem((4, 256, 1024), F32), vmem((4, DEVS, 2, 128), F32), vmem((128, 128), F32), vmem((128, 128), F32),
        vmem((128, 128), F32), vmem((1, 128), i32), vmem((1, 128), i32), vmem((1, 512), i32), vmem((1, 512), i32),
        vmem((1, 512), i32), vmem((1, 512), F32), vmem((DMAX, 512), F32), vmem((DMAX, 512), F32),
        vmem((16, 128, 8, 128), F32), vmem((128, 128, 128), F32), vmem((128, 128), F32), vmem((128, 128), F32),
        vmem((STEPS, 128, 128), F32), vmem((3, NETS, 1, 128), F32), vmem((3, NETS, 1, 128), F32),
        vmem((3, DEVS, 8, 512), F32), vmem((STEPS + 1, DEVS, 2, 8, 128), F32), vmem((16, 512), F32),
        vmem((16, 512), F32), vmem((6, 2, 1, 512), F32), vmem((6, 2, DEVS, 1, 512), F32),
        vmem((2, NETS, 1, 128), F32), vmem((2, NETS, 1, 128), F32), vmem((128, 1024), BF16),
        vmem((DEVS, 128, 512), BF16), vmem((DEVS, 8, 512), F32), vmem((4, 256, 128), F32),
        vmem((STEPS, DEVS, 8, 128), F32),
        dma((13,)), dma((16,)), dma((3, NETS)), dma((3, NETS)), dma((3, DEVS)), dma((3, DEVS)),
        dma((STEPS + 1, DEVS)), dma((STEPS + 1, DEVS)), dma((6, 2, DEVS)), dma((6, 2, DEVS)), dma, dma,
        dma((2, NETS)), dma((2, NETS)),
    ]
    v = pl.BlockSpec(memory_space=vmem)
    return pl.pallas_call(
        grid_kernel,
        out_shape=(jax.ShapeDtypeStruct((STEPS, 4096), F32), jax.ShapeDtypeStruct((128, 128), F32)),
        in_specs=[pl.BlockSpec(memory_space=pl.ANY)] * 14,
        out_specs=(v, v),
        scratch_shapes=scratch,
        compiler_params=pltpu.CompilerParams(collective_id=0, has_side_effects=True, vmem_limit_bytes=56 << 20),
    )(zinv, source.reshape(4, DEVS, 2, 128), model_state, propagator, input_gain, output_gain,
      model_owner.reshape(1, 128), model_bus.reshape(1, 128), line_from.reshape(1, 512), line_to.reshape(1, 512),
      line_delay.reshape(1, 512), line_imped.reshape(1, 512), wave_from_past, wave_to_past)


def solution(mesh):
    one_axis, both = P("net"), P(("net", "dev"))
    two = P(("net", "dev"), None)
    in_specs = (P("net", "dev", None), one_axis, two, P(("net", "dev"), None, None), two, two, two, both,
                one_axis, one_axis, one_axis, one_axis, P(None, "net"), P(None, "net"))
    return jax.shard_map(body, mesh=mesh, in_specs=in_specs, out_specs=(P(None, "net"), two), check_vma=False)
```

```python
import jax
import jax.numpy as jnp
from jax import lax
from jax.experimental import pallas as pl
from jax.experimental.pallas import tpu as pltpu
from jax.sharding import PartitionSpec as P

STEPS = 8
DMIN = 2
DMAX = 6
NETS = 32
DEVS = 4
CAP = 16
F32 = jnp.float32
BF16 = jnp.bfloat16
MESH = pl.DeviceIdType.MESH


def rows_sum(x):
    return jnp.sum(x, axis=0, keepdims=True)


def parts(x, count=3):
    pieces = []
    for i in range(count):
        piece = x.astype(BF16)
        pieces.append(piece)
        if i + 1 < count:
            x = x - piece.astype(F32)
    return pieces


def dot(a, b, dims):
    return lax.dot_general(a, b, (dims, ((), ())), preferred_element_type=F32)


def nn(a, b):
    return dot(a, b, ((1,), (0,)))


def nt(a, b):
    return dot(a, b, ((1,), (1,)))


def tn(a, b):
    return dot(a, b, ((0,), (0,)))


def iota(shape, dim):
    return lax.broadcasted_iota(jnp.int32, shape, dim)


def iota_f(shape, dim):
    return iota(shape, dim).astype(F32)


def one(mask):
    return jnp.where(mask, 1.0, 0.0).astype(F32)


def third_sum(x):
    rows = x.shape[0] // 3
    return x[:rows] + x[rows:2 * rows] + x[2 * rows:]


FAR_FIRST = sorted(range(1, NETS), key=lambda k: -min(k // 8, 4 - k // 8) - min(k // 2 % 4, 4 - k // 2 % 4) - k % 2)


def grid_kernel(zinv, source, state0, prop, bgain, ogain, owner_i, bus_i, from_i, to_i, delay_i, imped_i, fpast, tpast,
                trace, final,
                z, src, st, gi, go, own_v, bus_v, from_v, to_v, delay_v, imped_v, fp, tp,
                raw, at, xs, bs, xb, asend, arecv, vall, uv, pack, prev, wsend, wrecv, rsend, rrecv,
                ohl, hots, brow, acc, jl,
                in_s, raw_s, a_s, a_r, v_s, v_r, uv_s, uv_r, w_s, w_r, l_s, l_r, r_s, r_r):
    n = lax.axis_index("net")
    d = lax.axis_index("dev")

    x = n // 8
    y = (n // 2) % 4
    core = n % 2

    def net(k):
        return lax.rem(n + k, NETS)

    def away(k, way=1):
        kx, ky, kc = way * (k // 8) + 4, way * ((k // 2) % 4) + 4, k % 2
        return lax.rem(x + kx, 4) * 8 + lax.rem(y + ky, 4) * 2 + lax.rem(core + kc, 2)

    def dev(j):
        return lax.rem(d + j, DEVS)

    def copy(a, b, send, recv, to_net, to_dev):
        return pltpu.make_async_remote_copy(src_ref=a, dst_ref=b, send_sem=send, recv_sem=recv,
                                            device_id=(to_net, to_dev), device_id_type=MESH)

    pairs = [(state0, st), (bgain, gi), (ogain, go), (owner_i, own_v), (bus_i, bus_v), (from_i, from_v), (to_i, to_v),
             (delay_i, delay_v), (imped_i, imped_v), (fpast, fp), (tpast, tp), (source, src), (zinv, z)]
    loads = [pltpu.make_async_copy(a, b, in_s.at[i]) for i, (a, b) in enumerate(pairs)]

    def raw_copy(c):
        return pltpu.make_async_copy(prop.at[:, pl.ds(8 * c, 8), :], raw.at[c], raw_s.at[c])

    for load in loads[:11]:
        load.start()
    for c in range(16):
        raw_copy(c).start()
    for load in loads[11:]:
        load.start()

    bar = pltpu.get_barrier_semaphore()

    def greet(to_net, to_dev):
        pl.semaphore_signal(bar, inc=1, device_id=(to_net, to_dev), device_id_type=MESH)

    lax.fori_loop(1, NETS, lambda k, _: (greet(net(k), d), 0)[1], 0)
    for j in range(1, DEVS):
        greet(n, dev(j))
        greet(net(1), dev(j))
        greet(net(NETS - 1), dev(j))

    for load in loads[:11]:
        load.wait()
    owner = own_v[...].astype(F32)
    own_x = jnp.floor(owner * 0.125)
    own_y = jnp.floor((owner - 8.0 * own_x) * 0.5)
    own_c = owner - 8.0 * own_x - 2.0 * own_y

    def steps_to(to, at, size):
        gap = to - at.astype(F32)
        return jnp.where(gap < 0.0, gap + size, gap)

    offset = 8.0 * steps_to(own_x, x, 4.0) + 2.0 * steps_to(own_y, y, 4.0) + steps_to(own_c, core, 2.0)
    wide = jnp.broadcast_to(owner, (128, 128))
    earlier = one(wide.T == wide) * one(iota((128, 128), 0) < iota((128, 128), 1))
    rank = rows_sum(earlier)
    own = one(iota_f((NETS, 128), 0) == offset).astype(BF16)
    seat = one(iota_f((CAP, 128), 0) == rank)
    ogt = go[...].T
    go[...] = ogt
    first_x = st[...].T
    first_b = gi[...].T
    xs[...] = first_x
    bs[...] = first_b
    xb[0] = first_b
    free_m = [rows_sum(first_x * ogt)]
    gain_m = [rows_sum(first_b * ogt)]
    pack[0:1, :] = to_v[...].astype(F32)
    pack[1:2, :] = delay_v[...].astype(F32)
    pack[2:3, :] = imped_v[...]
    pack[3:9, :] = fp[...]
    pack[9:16, :] = jnp.zeros((7, 512), F32)

    flat = raw.reshape(16, 1024, 128)
    zero = jnp.zeros((128, 128), F32)

    def first(c, held):
        raw_copy(c).wait()
        ax, ab = held
        for kk in range(8):
            k = 8 * c + kk
            a = flat[c, pl.ds(kk, 128, stride=8), :].T
            at[k] = a
            ax = ax + a * xs[pl.ds(k, 1), :]
            ab = ab + a * bs[pl.ds(k, 1), :]
        return ax, ab

    def later(i, held):
        ax, ab = held
        for kk in range(8):
            k = 8 * i + kk
            a = at[k]
            ax = ax + a * xs[pl.ds(k, 1), :]
            ab = ab + a * bs[pl.ds(k, 1), :]
        return ax, ab

    def product(step):
        ax, ab = lax.fori_loop(0, 16, later if step else first, (zero, zero))
        xs[...] = ax
        if step + 1 < STEPS:
            bs[...] = ab
            xb[step + 1] = ab
            free_m.append(rows_sum(ax * go[...]))
            gain_m.append(rows_sum(ab * go[...]))

    def a_copy(b, k):
        return copy(asend.at[b, k], arecv.at[b, k], a_s.at[b], a_r.at[b], away(k), d)

    def a_all(b):
        rest = pl.ds(1, NETS - 1)
        return copy(asend.at[b, rest], arecv.at[b, rest], a_s.at[b], a_r.at[b], away(1), d)

    def send_batch(b, values):
        table = [value * seat for value in values]
        table.append(jnp.zeros((128 - CAP * len(values), 128), F32))
        packed = sum(nt(own, piece) for piece in parts(jnp.concatenate(table, axis=0)))
        asend[b, :, 0, :] = packed
        arecv[b, 0] = packed[0:1, :]
        for k in FAR_FIRST:
            a_copy(b, k).start()

    def v_copy(b, j):
        return copy(vall.at[b, d], vall.at[b, d], v_s.at[b, j], v_r.at[b, d], n, dev(j))

    def v_wait(b, j):
        return copy(vall.at[b, dev(j)], vall.at[b, dev(j)], v_s.at[b, j], v_r.at[b, dev(j)], n, dev(j))

    def share_batch(b):
        a_all(b).wait_recv()
        mask = one(iota((CAP, 128), 1) % CAP == iota((CAP, 128), 0))
        collect = one(iota((8, 128), 1) // CAP == iota((8, 128), 0)).astype(BF16)
        spread = jnp.concatenate([arecv[b, k] * mask for k in range(NETS)], axis=0)
        vall[b, d] = sum(nt(collect, piece) for piece in parts(spread))
        for j in range(1, DEVS):
            v_copy(b, j).start()

    row = iota((8, 1), 0)
    row_high = ((row // 2) * 8 + 2 * d + row % 2).astype(F32)
    row32 = iota((32, 1), 0)
    high32 = (((row32 % 8) // 2) * 8 + 2 * (row32 // 8) + row32 % 2).astype(F32)
    slot_high = []

    def place_batch(b):
        first_rows = 32 if b == 0 else 8
        count = 3 if b == 0 else 4
        total = jnp.zeros((3 * (first_rows + 8 * (count - 1)), 128), F32)
        for j in range(DEVS):
            if j:
                v_wait(b, j).wait_recv()
            vals = vall[b, dev(j)]
            if b == 0:
                bus = vals[3:4, :] - 1.0
                b_high = jnp.floor(bus * (1.0 / 128.0))
                slot_high.append(b_high)
                hots[j] = one(iota_f((128, 512), 0) == bus - 128.0 * b_high).astype(BF16)
                brow[j] = one(b_high == row_high)
            held = brow[j]
            whole = one(b_high == high32) if b == 0 else held
            left = jnp.concatenate([vals[0:1, :] * whole] + [vals[q:q + 1, :] * held for q in range(1, count)], axis=0)
            total = total + nt(jnp.concatenate(parts(left), axis=0), hots[j])
        total = third_sum(total)
        return [total[:first_rows]] + [total[first_rows + 8 * q:first_rows + 8 * q + 8] for q in range(count - 1)]

    product(0)
    pl.semaphore_wait(bar, NETS - 1 + 3 * (DEVS - 1))
    line_copy = copy(pack, prev, l_s, l_r, net(1), d)
    line_copy.start()
    send_batch(0, [free_m[0], free_m[1], gain_m[0], bus_v[...].astype(F32) + 1.0])
    product(1)
    product(2)
    send_batch(1, free_m[2:4] + gain_m[1:3])
    share_batch(0)

    line_copy.wait_recv()
    ends = jnp.concatenate([from_v[...].astype(F32), prev[0:1, :]], axis=1)
    delay = jnp.concatenate([pack[1:2, :], prev[1:2, :]], axis=1)
    twice = 2.0 / jnp.concatenate([pack[2:3, :], prev[2:3, :]], axis=1)
    waves = [jnp.concatenate([tp[i:i + 1, :], prev[3 + i:4 + i, :]], axis=1) for i in range(DMAX)]
    high = jnp.floor(ends * (1.0 / 128.0))
    ohl[...] = one(iota_f((128, 1024), 0) == ends - 128.0 * high).astype(BF16)
    mine = rows_sum(one(high == row_high))

    def arrivals(t):
        got = jnp.zeros((1, 1024), F32)
        for lag in range(DMIN, DMAX + 1):
            if DMAX + t - lag < len(waves):
                got = jnp.where(delay == float(lag), waves[DMAX + t - lag], got)
        return got

    def inject(t):
        left = jnp.concatenate(parts(one(high == high32) * arrive[t]), axis=0)
        jl[t] = third_sum(nt(left, ohl[...])).reshape(DEVS, 8, 128)

    def sample(v):
        left = jnp.concatenate(parts(v), axis=0)
        return rows_sum(third_sum(nn(left, ohl[...])) * one(high == row_high))

    arrive = [arrivals(0), arrivals(1)]
    inject(0)
    inject(1)

    def uv_copy(t, j):
        return copy(uv.at[t, d], uv.at[t, d], uv_s.at[t], uv_r.at[t, d], n, dev(j))

    def uv_wait(t, j):
        return copy(uv.at[t, dev(j)], uv.at[t, dev(j)], uv_s.at[t], uv_r.at[t, dev(j)], n, dev(j))

    def uv_all(t):
        sent = uv.at[t, pl.ds(0, DEVS - 1)]
        return copy(sent, sent, uv_s.at[t], uv_r.at[t, d], n, dev(1))

    def uv_send(t, u, v):
        uv[t, d, 0] = u
        uv[t, d, 1] = v
        for j in (2, 1, 3):
            uv_copy(t, j).start()

    def w_copy(t, way, j):
        return copy(wsend.at[t, way], wrecv.at[t, way, d], w_s.at[t], w_r.at[t], net(1 if way == 0 else NETS - 1), dev(j))

    def w_all(t):
        return copy(wrecv.at[t], wrecv.at[t], w_s.at[t], w_r.at[t], net(1), d)

    def send_waves(t):
        wave = mine * (sample(volts[t]) * twice - arrive[t])
        wsend[t, 0] = wave[:, :512]
        wsend[t, 1] = wave[:, 512:]
        for j in (2, 1, 3, 0):
            for way in range(2):
                w_copy(t, way, j).start()

    def take_waves(t):
        w_all(t).wait_recv()
        waves.append(jnp.concatenate([sum(wrecv[t, 1, j] for j in range(DEVS)),
                                      sum(wrecv[t, 0, j] for j in range(DEVS))], axis=1))
        arrive.append(arrivals(t + DMIN))
        inject(t + DMIN)

    def columns(t, c, s):
        tiles = uv[t, c, 0] + jl[t, c]
        total = None
        for e in range(2):
            lanes = pl.ds(pl.multiple_of(256 * c + 128 * e, 128), 128)
            term = z[s, :, lanes] * tiles[2 * s + e:2 * s + e + 1, :]
            total = term if total is None else total + term
        return total

    def solve(t):
        if t:
            uv_wait(t, 1).wait_recv()
            uv_wait(t, 3).wait_recv()
        for s in range(4):
            acc[s] = columns(t, d, s) + columns(t, dev(1), s) + columns(t, dev(3), s)
        if t:
            uv_wait(t, 2).wait_recv()
        rows = []
        for s in range(4):
            total = acc[s] + columns(t, dev(2), s)
            rows.append(rows_sum(total[:128].T))
            rows.append(rows_sum(total[128:].T))
        return jnp.concatenate(rows, axis=0)

    def keep(t):
        for c in range(8):
            for s in range(4):
                spot = 1024 * s + 128 * c
                trace[t:t + 1, spot:spot + 128] = uv[t + 1, c // 2, 1, 2 * s + c % 2:2 * s + c % 2 + 1, :]

    def r_copy(b, k):
        return copy(rsend.at[b, k], rrecv.at[b, k], r_s.at[b], r_r.at[b], away(k, -1), d)

    def r_all(b):
        rest = pl.ds(1, NETS - 1)
        return copy(rsend.at[b, rest], rrecv.at[b, rest], r_s.at[b], r_r.at[b], away(1), d)

    def send_back(b, steps):
        full = jnp.concatenate([uv[t + 1, c, 1] for t in steps for c in range(DEVS)], axis=0)
        reached = sum(nn(piece, hots[0]) for piece in parts(full))
        pick = one(slot_high[0] == high32)
        seats = one(iota((CAP, 512), 1) % CAP == iota((CAP, 512), 0))
        home = one(iota((NETS, 512), 1) // CAP == iota((NETS, 512), 0)).astype(BF16)
        table = [rows_sum(reached[32 * i:32 * i + 32] * pick) * seats for i in range(len(steps))]
        table.append(jnp.zeros((128 - CAP * len(steps), 512), F32))
        back = sum(nt(home, piece) for piece in parts(jnp.concatenate(table, axis=0)))
        rsend[b, :, 0, :] = back
        rrecv[b, 0] = back[0:1, :]
        for k in FAR_FIRST:
            r_copy(b, k).start()

    def at_models(b):
        r_all(b).wait_recv()
        return parts(rrecv[b, :, 0, :])

    product(3)
    product(4)
    free, gain, volts = [], [], []
    got = place_batch(0)
    free += got[:2]
    gain += got[2:]
    for load in loads[11:]:
        load.wait()
    for c in range(DEVS):
        uv[0, c, 0] = jnp.concatenate([src[s, c] for s in range(4)], axis=0) + free[0][8 * c:8 * c + 8]
    base = jnp.concatenate([src[s, d] for s in range(4)], axis=0)
    for t in range(STEPS):
        if t == 1:
            share_batch(1)
        if 1 <= t <= STEPS - DMIN:
            send_waves(t - 1)
        if t == 1:
            send_batch(2, free_m[4:6] + gain_m[3:5])
        if t == 2:
            product(5)
        if t == 3:
            product(6)
            send_batch(3, free_m[6:8] + gain_m[5:7])
        if t == 4:
            product(7)
        if t >= 2:
            take_waves(t - 2)
        if t == 2:
            share_batch(2)
        if t == 4:
            share_batch(3)
        if t % 2:
            got = place_batch((t + 1) // 2) if t < 7 else []
            free += got[:2]
            gain += got[2:]
        if t >= 5:
            for old in ((0, 1), (2, 3), (4, 5))[t - 5]:
                keep(old)
        ready = base
        if t + 1 < STEPS:
            ready = ready + free[t + 1]
            for k in range(t):
                ready = ready + gain[t - k] * volts[k]
        v = solve(t)
        volts.append(v)
        uv_send(t + 1, ready + gain[0] * v if t + 1 < STEPS else jnp.zeros((8, 128), F32), v)
    send_back(0, list(range(STEPS - 1)))
    for j in range(1, DEVS):
        uv_wait(STEPS, j).wait_recv()
    send_back(1, [STEPS - 1])

    keep(STEPS - 2)
    keep(STEPS - 1)
    line_copy.wait_send()
    for b in range(4):
        a_all(b).wait_send()
        for j in range(1, DEVS):
            v_copy(b, j).wait_send()
    for t in range(1, STEPS + 1):
        uv_all(t).wait_send()
    for t in range(STEPS - DMIN):
        w_all(t).wait_send()
    state = xs[...]
    by_seat = sum(tn(piece, own) for piece in at_models(0))
    for t in range(STEPS - 1):
        state = state + rows_sum(by_seat[CAP * t:CAP * t + CAP] * seat) * xb[STEPS - 1 - t]
    state = state.T
    seat_cols = jnp.concatenate([seat, jnp.zeros((128 - CAP, 128), F32)], axis=0).T
    for b in range(2):
        r_all(b).wait_send()
    by_model = sum(tn(own, piece) for piece in at_models(1))
    final[...] = state + jnp.sum(by_model * seat_cols, axis=1, keepdims=True) * gi[...]


def body(zinv, source, model_state, propagator, input_gain, output_gain, model_owner, model_bus,
         line_from, line_to, line_delay, line_imped, wave_from_past, wave_to_past):
    vmem, dma = pltpu.VMEM, pltpu.SemaphoreType.DMA
    i32 = jnp.int32
    scratch = [
        vmem((4, 256, 1024), F32), vmem((4, DEVS, 2, 128), F32), vmem((128, 128), F32), vmem((128, 128), F32),
        vmem((128, 128), F32), vmem((1, 128), i32), vmem((1, 128), i32), vmem((1, 512), i32), vmem((1, 512), i32),
        vmem((1, 512), i32), vmem((1, 512), F32), vmem((DMAX, 512), F32), vmem((DMAX, 512), F32),
        vmem((16, 128, 8, 128), F32), vmem((128, 128, 128), F32), vmem((128, 128), F32), vmem((128, 128), F32),
        vmem((STEPS, 128, 128), F32), vmem((4, NETS, 1, 128), F32), vmem((4, NETS, 1, 128), F32),
        vmem((4, DEVS, 8, 512), F32), vmem((STEPS + 1, DEVS, 2, 8, 128), F32), vmem((16, 512), F32),
        vmem((16, 512), F32), vmem((6, 2, 1, 512), F32), vmem((6, 2, DEVS, 1, 512), F32),
        vmem((2, NETS, 1, 128), F32), vmem((2, NETS, 1, 128), F32), vmem((128, 1024), BF16),
        vmem((DEVS, 128, 512), BF16), vmem((DEVS, 8, 512), F32), vmem((4, 256, 128), F32),
        vmem((STEPS, DEVS, 8, 128), F32),
        dma((13,)), dma((16,)), dma((4,)), dma((4,)), dma((4, DEVS)), dma((4, DEVS)),
        dma((STEPS + 1,)), dma((STEPS + 1, DEVS)), dma((6,)), dma((6,)), dma, dma, dma((2,)), dma((2,)),
    ]
    v = pl.BlockSpec(memory_space=vmem)
    return pl.pallas_call(
        grid_kernel,
        out_shape=(vmem((STEPS, 4096), F32), vmem((128, 128), F32)),
        in_specs=[pl.BlockSpec(memory_space=pl.ANY)] * 14,
        out_specs=(v, v),
        scratch_shapes=scratch,
        compiler_params=pltpu.CompilerParams(collective_id=0, has_side_effects=True, vmem_limit_bytes=56 << 20),
    )(zinv, source.reshape(4, DEVS, 2, 128), model_state, propagator, input_gain, output_gain,
      model_owner.reshape(1, 128), model_bus.reshape(1, 128), line_from.reshape(1, 512), line_to.reshape(1, 512),
      line_delay.reshape(1, 512), line_imped.reshape(1, 512), wave_from_past, wave_to_past)


def solution(mesh):
    one_axis, both = P("net"), P(("net", "dev"))
    two = P(("net", "dev"), None)
    in_specs = (P("net", "dev", None), one_axis, two, P(("net", "dev"), None, None), two, two, two, both,
                one_axis, one_axis, one_axis, one_axis, P(None, "net"), P(None, "net"))
    return jax.shard_map(body, mesh=mesh, in_specs=in_specs, out_specs=(P(None, "net"), two), check_vma=False)
```

```python
import jax
import jax.numpy as jnp
from jax import lax
from jax.experimental import pallas as pl
from jax.experimental.pallas import tpu as pltpu
from jax.sharding import PartitionSpec as P

STEPS = 8
DMIN = 2
DMAX = 6
NETS = 32
DEVS = 4
CAP = 16
PARTS = 2
F32 = jnp.float32
BF16 = jnp.bfloat16
MESH = pl.DeviceIdType.MESH


def rows_sum(x):
    return jnp.sum(x, axis=0, keepdims=True)


def parts(x, count=PARTS):
    pieces = []
    for i in range(count):
        piece = x.astype(BF16)
        pieces.append(piece)
        if i + 1 < count:
            x = x - piece.astype(F32)
    return pieces


def dot(a, b, dims):
    return lax.dot_general(a, b, (dims, ((), ())), preferred_element_type=F32)


def nn(a, b):
    return dot(a, b, ((1,), (0,)))


def nt(a, b):
    return dot(a, b, ((1,), (1,)))


def tn(a, b):
    return dot(a, b, ((0,), (0,)))


def iota(shape, dim):
    return lax.broadcasted_iota(jnp.int32, shape, dim)


def iota_f(shape, dim):
    return iota(shape, dim).astype(F32)


def one(mask):
    return jnp.where(mask, 1.0, 0.0).astype(F32)


def add_parts(x):
    rows = x.shape[0] // PARTS
    return sum(x[rows * i:rows * i + rows] for i in range(PARTS))


def hops(k):
    x, y, z = (min(v, 4 - v) for v in (k // 8 % 4, k // 2 % 4, k // 32))
    return x + y + z + k % 2 * 0.5


FAR_FIRST = sorted(range(1, NETS), key=hops, reverse=True)
ALL_FAR_FIRST = sorted(range(1, NETS * DEVS), key=hops, reverse=True)


def grid_kernel(zinv, source, state0, prop, bgain, ogain, owner_i, bus_i, from_i, to_i, delay_i, imped_i, fpast, tpast,
                trace, final,
                z, src, st, gi, go, own_v, bus_v, from_v, to_v, delay_v, imped_v, fp, tp,
                raw, at, xp, xb, rp, asend, arecv, arecv0, vall, uv, pack, prev, wsend, wrecv, rsend, rrecv, lsend, lrecv,
                ohl, hots, brow, acc, jl,
                in_s, raw_s, a_s, a_r, v_s, v_r, uv_s, uv_r, w_s, w_r, l_s, l_r, r_s, r_r, e_s, e_r):
    n = lax.axis_index("net")
    d = lax.axis_index("dev")

    x = n // 8
    y = (n // 2) % 4
    core = n % 2

    def net(k):
        return lax.rem(n + k, NETS)

    def away(k, way=1):
        kx, ky, kc = way * (k // 8) + 4, way * ((k // 2) % 4) + 4, k % 2
        return lax.rem(x + kx, 4) * 8 + lax.rem(y + ky, 4) * 2 + lax.rem(core + kc, 2)

    def dev(j):
        return lax.rem(d + j, DEVS)

    def copy(a, b, send, recv, to_net, to_dev):
        return pltpu.make_async_remote_copy(src_ref=a, dst_ref=b, send_sem=send, recv_sem=recv,
                                            device_id=(to_net, to_dev), device_id_type=MESH)

    pairs = [(state0, st), (bgain, gi), (ogain, go), (owner_i, own_v), (bus_i, bus_v), (from_i, from_v), (to_i, to_v),
             (delay_i, delay_v), (imped_i, imped_v), (fpast, fp), (tpast, tp), (source, src), (zinv, z)]
    loads = [pltpu.make_async_copy(a, b, in_s.at[i]) for i, (a, b) in enumerate(pairs)]

    def raw_copy(c):
        return pltpu.make_async_copy(prop.at[:, pl.ds(8 * c, 8), :], raw.at[c], raw_s.at[c])

    for load in loads[:11]:
        load.start()
    for c in range(16):
        raw_copy(c).start()
    for load in loads[11:]:
        load.start()

    bar = pltpu.get_barrier_semaphore()

    def greet(to_net, to_dev):
        pl.semaphore_signal(bar, inc=1, device_id=(to_net, to_dev), device_id_type=MESH)

    def greet_all(k, _):
        for j in range(DEVS):
            greet(net(k), dev(j))
        return 0

    lax.fori_loop(1, NETS, greet_all, 0)
    for j in range(1, DEVS):
        greet(n, dev(j))

    for load in loads[:11]:
        load.wait()
    owner = own_v[...].astype(F32)
    own_x = jnp.floor(owner * 0.125)
    own_y = jnp.floor((owner - 8.0 * own_x) * 0.5)
    own_c = owner - 8.0 * own_x - 2.0 * own_y

    def steps_to(to, at, size):
        gap = to - at.astype(F32)
        return jnp.where(gap < 0.0, gap + size, gap)

    offset = 8.0 * steps_to(own_x, x, 4.0) + 2.0 * steps_to(own_y, y, 4.0) + steps_to(own_c, core, 2.0)
    wide = jnp.broadcast_to(owner, (128, 128))
    earlier = one(wide.T == wide) * one(iota((128, 128), 0) < iota((128, 128), 1))
    rank = rows_sum(earlier)
    own = one(iota_f((NETS, 128), 0) == offset).astype(BF16)
    seat = one(iota_f((CAP, 128), 0) == rank)
    xp[0] = st[...].T
    xb[0] = gi[...].T
    rp[0] = go[...].T
    pack[0:1, :] = to_v[...].astype(F32)
    pack[1:2, :] = delay_v[...].astype(F32)
    pack[2:3, :] = imped_v[...]
    pack[3:9, :] = fp[...]
    pack[9:16, :] = jnp.zeros((7, 512), F32)

    flat = raw.reshape(16, 1024, 128)
    zero = jnp.zeros((128, 128), F32)

    def passes(i, x=None, b=None, r=None):
        def group(c, held):
            ax, ab = held
            if not i:
                raw_copy(c).wait()
            rows = []
            for kk in range(8):
                k = 8 * c + kk
                if i:
                    a = at[k]
                else:
                    a = flat[c, pl.ds(kk, 128, stride=8), :].T
                    at[k] = a
                if x is not None:
                    ax = ax + a * xp[x, pl.ds(k, 1), :]
                if b is not None:
                    ab = ab + a * xb[b, pl.ds(k, 1), :]
                if r is not None:
                    rows.append(rows_sum(a * rp[r]))
            if r is not None:
                rp[r + 1, pl.ds(8 * c, 8), :] = jnp.concatenate(rows, axis=0)
            return ax, ab

        ax, ab = lax.fori_loop(0, 16, group, (zero if x is not None else 0, zero if b is not None else 0))
        if x is not None:
            xp[x + 1] = ax
        if b is not None:
            xb[b + 1] = ab

    def free_of(i, j):
        return rows_sum(xp[i] * rp[j])

    def gain_of(i, j):
        return rows_sum(xb[i] * rp[j])

    def a_copy(b, k):
        return copy(asend.at[b, k], arecv.at[b, k], a_s.at[b], a_r.at[b], away(k), d)

    def a_all(b):
        rest = pl.ds(1, NETS - 1)
        return copy(asend.at[b, rest], arecv.at[b, rest], a_s.at[b], a_r.at[b], away(1), d)

    def first_copy(g):
        return copy(asend.at[0, g % NETS], arecv0.at[g], a_s.at[0], a_r.at[0], away(g % NETS), dev(g // NETS))

    def first_all():
        rest = pl.ds(1, NETS * DEVS - 1)
        return copy(arecv0.at[rest], arecv0.at[rest], a_s.at[0], a_r.at[0], away(1), d)

    def send_batch(b, values):
        table = [value * seat for value in values]
        if len(values) < 8:
            table.append(jnp.zeros((128 - CAP * len(values), 128), F32))
        packed = sum(nt(own, piece) for piece in parts(jnp.concatenate(table, axis=0)))
        asend[b, :, 0, :] = packed
        if b:
            arecv[b, 0] = packed[0:1, :]
            for k in FAR_FIRST:
                a_copy(b, k).start()
        else:
            arecv0[0] = packed[0:1, :]
            for g in ALL_FAR_FIRST:
                first_copy(g).start()

    def v_copy(b, j):
        return copy(vall.at[b, d], vall.at[b, d], v_s.at[b, j], v_r.at[b, d], n, dev(j))

    def v_wait(b, j):
        return copy(vall.at[b, dev(j)], vall.at[b, dev(j)], v_s.at[b, j], v_r.at[b, dev(j)], n, dev(j))

    def unpack(ref, at):
        mask = one(iota((CAP, 128), 1) % CAP == iota((CAP, 128), 0))
        collect = one(iota((8, 128), 1) // CAP == iota((8, 128), 0)).astype(BF16)
        spread = jnp.concatenate([ref[at + k] * mask for k in range(NETS)], axis=0)
        return sum(nt(collect, piece) for piece in parts(spread))

    def share_batch(b):
        a_all(b).wait_recv()
        vall[b, d] = unpack(arecv.at[b], 0)
        for j in range(1, DEVS):
            v_copy(b, j).start()

    row = iota((8, 1), 0)
    row_high = ((row // 2) * 8 + 2 * d + row % 2).astype(F32)
    row32 = iota((32, 1), 0)
    high32 = (((row32 % 8) // 2) * 8 + 2 * (row32 // 8) + row32 % 2).astype(F32)
    slot_high = []

    def place_batch(b, count):
        first_rows = 8 if b else 32
        total = 0.0
        for j in range(DEVS):
            if b:
                if j:
                    v_wait(b, j).wait_recv()
                vals = vall[b, dev(j)]
                whole = brow[j]
            else:
                vals = unpack(arecv0, NETS * ((DEVS - j) % DEVS))
                bus = vals[7:8, :] - 1.0
                b_high = jnp.floor(bus * (1.0 / 128.0))
                slot_high.append(b_high)
                hots[j] = one(iota_f((128, 512), 0) == bus - 128.0 * b_high).astype(BF16)
                brow[j] = one(b_high == row_high)
                whole = one(b_high == high32)
            left = jnp.concatenate([vals[0:1, :] * whole] + [vals[q:q + 1, :] * brow[j] for q in range(1, count)], axis=0)
            total = total + nt(jnp.concatenate(parts(left), axis=0), hots[j])
        total = add_parts(total)
        return [total[:first_rows]] + [total[first_rows + 8 * q:first_rows + 8 * q + 8] for q in range(count - 1)]

    passes(0, x=0, b=0, r=0)
    passes(1, x=1)
    pl.semaphore_wait(bar, NETS * DEVS - 1)
    line_copy = copy(pack, prev, l_s, l_r, net(1), d)
    line_copy.start()
    send_batch(0, [free_of(0, 0), free_of(1, 0), free_of(1, 1), free_of(2, 1),
                   gain_of(0, 0), gain_of(1, 0), gain_of(1, 1), bus_v[...].astype(F32) + 1.0])

    line_copy.wait_recv()
    ends = jnp.concatenate([from_v[...].astype(F32), prev[0:1, :]], axis=1)
    delay = jnp.concatenate([pack[1:2, :], prev[1:2, :]], axis=1)
    twice = 2.0 / jnp.concatenate([pack[2:3, :], prev[2:3, :]], axis=1)
    waves = [jnp.concatenate([tp[i:i + 1, :], prev[3 + i:4 + i, :]], axis=1) for i in range(DMAX)]
    high = jnp.floor(ends * (1.0 / 128.0))
    ohl[...] = one(iota_f((128, 1024), 0) == ends - 128.0 * high).astype(BF16)
    mine = rows_sum(one(high == row_high))

    def arrivals(t):
        got = jnp.zeros((1, 1024), F32)
        for lag in range(DMIN, DMAX + 1):
            if DMAX + t - lag < len(waves):
                got = jnp.where(delay == float(lag), waves[DMAX + t - lag], got)
        return got

    def inject(t):
        left = jnp.concatenate(parts(one(high == high32) * arrive[t]), axis=0)
        jl[t] = add_parts(nt(left, ohl[...])).reshape(DEVS, 8, 128)

    def sample(v):
        left = jnp.concatenate(parts(v), axis=0)
        return rows_sum(add_parts(nn(left, ohl[...])) * one(high == row_high))

    arrive = [arrivals(0), arrivals(1)]
    inject(0)
    inject(1)

    def uv_copy(t, j):
        return copy(uv.at[t, d], uv.at[t, d], uv_s.at[t], uv_r.at[t, d], n, dev(j))

    def uv_wait(t, j):
        return copy(uv.at[t, dev(j)], uv.at[t, dev(j)], uv_s.at[t], uv_r.at[t, dev(j)], n, dev(j))

    def uv_all(t):
        sent = uv.at[t, pl.ds(0, DEVS - 1)]
        return copy(sent, sent, uv_s.at[t], uv_r.at[t, d], n, dev(1))

    def uv_send(t, u, v):
        uv[t, d, 0] = u
        uv[t, d, 1] = v
        for j in (2, 1, 3):
            uv_copy(t, j).start()

    def w_copy(t, way, j):
        return copy(wsend.at[t, way], wrecv.at[t, way, d], w_s.at[t], w_r.at[t], net(1 if way == 0 else NETS - 1), dev(j))

    def w_all(t):
        return copy(wrecv.at[t], wrecv.at[t], w_s.at[t], w_r.at[t], net(1), d)

    def send_waves(t):
        wave = mine * (sample(volts[t]) * twice - arrive[t])
        wsend[t, 0] = wave[:, :512]
        wsend[t, 1] = wave[:, 512:]
        for j in (2, 1, 3, 0):
            for way in range(2):
                w_copy(t, way, j).start()

    def take_waves(t):
        w_all(t).wait_recv()
        waves.append(jnp.concatenate([sum(wrecv[t, 1, j] for j in range(DEVS)),
                                      sum(wrecv[t, 0, j] for j in range(DEVS))], axis=1))
        arrive.append(arrivals(t + DMIN))
        inject(t + DMIN)

    def columns(t, c, s):
        tiles = uv[t, c, 0] + jl[t, c]
        total = None
        for e in range(2):
            lanes = pl.ds(pl.multiple_of(256 * c + 128 * e, 128), 128)
            term = z[s, :, lanes] * tiles[2 * s + e:2 * s + e + 1, :]
            total = term if total is None else total + term
        return total

    def solve(t):
        if t:
            uv_wait(t, 1).wait_recv()
            uv_wait(t, 3).wait_recv()
        for s in range(4):
            acc[s] = columns(t, d, s) + columns(t, dev(1), s) + columns(t, dev(3), s)
        if t:
            uv_wait(t, 2).wait_recv()
        rows = []
        for s in range(4):
            total = acc[s] + columns(t, dev(2), s)
            rows.append(rows_sum(total[:128].T))
            rows.append(rows_sum(total[128:].T))
        return jnp.concatenate(rows, axis=0)

    def keep(t):
        for c in range(8):
            for s in range(4):
                spot = 1024 * s + 128 * c
                trace[t:t + 1, spot:spot + 128] = uv[t + 1, c // 2, 1, 2 * s + c % 2:2 * s + c % 2 + 1, :]

    def r_copy(b, k):
        return copy(rsend.at[b, k], rrecv.at[b, k], r_s.at[b], r_r.at[b], away(k, -1), d)

    def r_all(b):
        rest = pl.ds(1, NETS - 1)
        return copy(rsend.at[b, rest], rrecv.at[b, rest], r_s.at[b], r_r.at[b], away(1), d)

    def send_back(b, steps):
        full = jnp.concatenate([uv[t + 1, c, 1] for t in steps for c in range(DEVS)], axis=0)
        reached = sum(nn(piece, hots[0]) for piece in parts(full))
        pick = one(slot_high[0] == high32)
        seats = one(iota((CAP, 512), 1) % CAP == iota((CAP, 512), 0))
        home = one(iota((NETS, 512), 1) // CAP == iota((NETS, 512), 0)).astype(BF16)
        table = [rows_sum(reached[32 * i:32 * i + 32] * pick) * seats for i in range(len(steps))]
        table.append(jnp.zeros((128 - CAP * len(steps), 512), F32))
        back = sum(nt(home, piece) for piece in parts(jnp.concatenate(table, axis=0)))
        rsend[b, :, 0, :] = back
        rrecv[b, 0] = back[0:1, :]
        for k in FAR_FIRST:
            r_copy(b, k).start()

    def last_copy(g):
        return copy(lsend.at[g // NETS, g % NETS // 8], lrecv.at[g], e_s, e_r, away(g % NETS, -1), dev(g // NETS))

    def last_all():
        rest = pl.ds(1, NETS * DEVS - 1)
        return copy(lrecv.at[rest], lrecv.at[rest], e_s, e_r, away(1), d)

    def send_last(early, late):
        left = jnp.concatenate(parts(jnp.concatenate([early, late], axis=0)), axis=0)
        for j in range(DEVS):
            found = add_parts(nn(left, hots[j]))
            for i in range(2):
                line = rows_sum(found[8 * i:8 * i + 8] * brow[j])
                for g in range(4):
                    lsend[j, g, i:i + 1, :] = line[:, 128 * g:128 * g + 128]
        lrecv[0] = lsend[0, 0]
        for g in ALL_FAR_FIRST:
            last_copy(g).start()

    free, gain, volts = [], [], []
    passes(2, b=1, r=1)
    first_all().wait_recv()
    got = place_batch(0, 7)
    free += got[:4]
    gain += got[4:]
    for load in loads[11:]:
        load.wait()
    for c in range(DEVS):
        uv[0, c, 0] = jnp.concatenate([src[s, c] for s in range(4)], axis=0) + free[0][8 * c:8 * c + 8]
    base = jnp.concatenate([src[s, d] for s in range(4)], axis=0)
    for t in range(STEPS):
        if 1 <= t <= STEPS - DMIN:
            send_waves(t - 1)
        if t == 1:
            send_batch(1, [free_of(2, 2), gain_of(1, 2), gain_of(2, 2)])
            passes(3, x=2, b=2, r=2)
        if t == 2:
            passes(4, x=3)
            send_batch(2, [free_of(3, 2), free_of(3, 3), free_of(4, 3), gain_of(3, 2), gain_of(3, 3)])
        if t >= 2:
            take_waves(t - 2)
        if t == 2:
            share_batch(1)
        if t == 3:
            got = place_batch(1, 3)
            free += got[:1]
            gain += got[1:]
            passes(5, x=4)
            share_batch(2)
        if t == 4:
            passes(6, x=5)
            got = place_batch(2, 5)
            free += got[:3]
            gain += got[3:]
        if t == 5:
            passes(7, x=6, b=3)
        if t == 6:
            passes(8, x=7, b=4)
        if t == 7:
            send_back(0, list(range(STEPS - 2)))
        ready = base
        if t + 1 < STEPS:
            ready = ready + free[t + 1]
            for k in range(t):
                ready = ready + gain[t - k] * volts[k]
        v = solve(t)
        volts.append(v)
        uv_send(t + 1, ready + gain[0] * v if t + 1 < STEPS else jnp.zeros((8, 128), F32), v)
    send_last(volts[-2], volts[-1])

    passes(9, b=5)
    passes(10, b=6)
    for t in range(STEPS - 1):
        keep(t)
    line_copy.wait_send()
    first_all().wait_send()
    for b in range(1, 3):
        a_all(b).wait_send()
        for j in range(1, DEVS):
            v_copy(b, j).wait_send()
    for t in range(1, STEPS + 1):
        uv_all(t).wait_send()
    for t in range(STEPS - DMIN):
        w_all(t).wait_send()
    r_all(0).wait_recv()
    by_seat = sum(tn(piece, own) for piece in parts(rrecv[0, :, 0, :]))
    state = xp[8]
    for t in range(STEPS - 2):
        state = state + rows_sum(by_seat[CAP * t:CAP * t + CAP] * seat) * xb[STEPS - 1 - t]
    state = state.T
    next_gain = xb[1].T
    spot = CAP * (offset - 8.0 * jnp.floor(offset * 0.125)) + rank
    spots = one(iota_f((128, 128), 0) == spot).T
    r_all(0).wait_send()
    for j in range(1, DEVS):
        uv_wait(STEPS, j).wait_recv()
    keep(STEPS - 1)
    last_all().wait_recv()
    columns_of = []
    for i in range(2):
        answer = sum(lrecv[NETS * j:NETS * j + NETS, i, :] for j in range(DEVS))
        by_model = sum(tn(own, piece) for piece in parts(answer))
        columns_of.append(jnp.sum(by_model * spots, axis=1, keepdims=True))
    final[...] = state + columns_of[0] * next_gain + columns_of[1] * gi[...]
    last_all().wait_send()


def body(zinv, source, model_state, propagator, input_gain, output_gain, model_owner, model_bus,
         line_from, line_to, line_delay, line_imped, wave_from_past, wave_to_past):
    vmem, dma = pltpu.VMEM, pltpu.SemaphoreType.DMA
    i32 = jnp.int32
    scratch = [
        vmem((4, 256, 1024), F32), vmem((4, DEVS, 2, 128), F32), vmem((128, 128), F32), vmem((128, 128), F32),
        vmem((128, 128), F32), vmem((1, 128), i32), vmem((1, 128), i32), vmem((1, 512), i32), vmem((1, 512), i32),
        vmem((1, 512), i32), vmem((1, 512), F32), vmem((DMAX, 512), F32), vmem((DMAX, 512), F32),
        vmem((16, 128, 8, 128), F32), vmem((128, 128, 128), F32), vmem((STEPS + 1, 128, 128), F32),
        vmem((STEPS, 128, 128), F32), vmem((4, 128, 128), F32), vmem((3, NETS, 1, 128), F32),
        vmem((3, NETS, 1, 128), F32), vmem((NETS * DEVS, 1, 128), F32), vmem((3, DEVS, 8, 512), F32), vmem((STEPS + 1, DEVS, 2, 8, 128), F32), vmem((16, 512), F32),
        vmem((16, 512), F32), vmem((6, 2, 1, 512), F32), vmem((6, 2, DEVS, 1, 512), F32),
        vmem((1, NETS, 1, 128), F32), vmem((1, NETS, 1, 128), F32),
        vmem((DEVS, 4, 2, 128), F32), vmem((NETS * DEVS, 2, 128), F32), vmem((128, 1024), BF16),
        vmem((DEVS, 128, 512), BF16), vmem((DEVS, 8, 512), F32), vmem((4, 256, 128), F32),
        vmem((STEPS, DEVS, 8, 128), F32),
        dma((13,)), dma((16,)), dma((3,)), dma((3,)), dma((3, DEVS)), dma((3, DEVS)),
        dma((STEPS + 1,)), dma((STEPS + 1, DEVS)), dma((6,)), dma((6,)), dma, dma, dma((1,)), dma((1,)), dma, dma,
    ]
    v = pl.BlockSpec(memory_space=vmem)
    return pl.pallas_call(
        grid_kernel,
        out_shape=(vmem((STEPS, 4096), F32), vmem((128, 128), F32)),
        in_specs=[pl.BlockSpec(memory_space=pl.ANY)] * 14,
        out_specs=(v, v),
        scratch_shapes=scratch,
        compiler_params=pltpu.CompilerParams(collective_id=0, has_side_effects=True, vmem_limit_bytes=56 << 20),
    )(zinv, source.reshape(4, DEVS, 2, 128), model_state, propagator, input_gain, output_gain,
      model_owner.reshape(1, 128), model_bus.reshape(1, 128), line_from.reshape(1, 512), line_to.reshape(1, 512),
      line_delay.reshape(1, 512), line_imped.reshape(1, 512), wave_from_past, wave_to_past)


def solution(mesh):
    one_axis, both = P("net"), P(("net", "dev"))
    two = P(("net", "dev"), None)
    in_specs = (P("net", "dev", None), one_axis, two, P(("net", "dev"), None, None), two, two, two, both,
                one_axis, one_axis, one_axis, one_axis, P(None, "net"), P(None, "net"))
    return jax.shard_map(body, mesh=mesh, in_specs=in_specs, out_specs=(P(None, "net"), two), check_vma=False)
```

```python
import jax
import jax.numpy as jnp
from jax import lax
from jax.experimental import pallas as pl
from jax.experimental.pallas import tpu as pltpu
from jax.sharding import PartitionSpec as P

STEPS = 8
DMIN = 2
DMAX = 6
NETS = 32
DEVS = 4
CAP = 16
PARTS = 2
F32 = jnp.float32
BF16 = jnp.bfloat16
MESH = pl.DeviceIdType.MESH


def rows_sum(x):
    return jnp.sum(x, axis=0, keepdims=True)


def parts(x, count=PARTS):
    pieces = []
    for i in range(count):
        piece = x.astype(BF16)
        pieces.append(piece)
        if i + 1 < count:
            x = x - piece.astype(F32)
    return pieces


def dot(a, b, dims):
    return lax.dot_general(a, b, (dims, ((), ())), preferred_element_type=F32)


def nn(a, b):
    return dot(a, b, ((1,), (0,)))


def nt(a, b):
    return dot(a, b, ((1,), (1,)))


def tn(a, b):
    return dot(a, b, ((0,), (0,)))


def iota(shape, dim):
    return lax.broadcasted_iota(jnp.int32, shape, dim)


def iota_f(shape, dim):
    return iota(shape, dim).astype(F32)


def one(mask):
    return jnp.where(mask, 1.0, 0.0).astype(F32)


def add_parts(x):
    rows = x.shape[0] // PARTS
    return sum(x[rows * i:rows * i + rows] for i in range(PARTS))


def hops(k):
    x, y, z = (min(v, 4 - v) for v in (k // 8 % 4, k // 2 % 4, k // 32))
    return x + y + z + k % 2 * 0.5


FAR_FIRST = sorted(range(1, NETS), key=hops, reverse=True)
ALL_FAR_FIRST = sorted(range(1, NETS * DEVS), key=hops, reverse=True)


def grid_kernel(zinv, source, state0, prop, bgain, ogain, owner_i, bus_i, from_i, to_i, delay_i, imped_i, fpast, tpast,
                trace, final,
                z, src, st, gi, go, own_v, bus_v, from_v, to_v, delay_v, imped_v, fp, tp,
                raw, at, xp, xb, rp, asend, arecv, arecv0, vall, um, vv, pack, prev, wsend, wrecv, rsend, rrecv, lsend, lrecv,
                ohl, hots, brow, acc, jl,
                in_s, raw_s, a_s, a_r, v_s, v_r, um_s, um_r, vv_s, vv_r, w_s, w_r, l_s, l_r, r_s, r_r, e_s, e_r):
    n = lax.axis_index("net")
    d = lax.axis_index("dev")

    x = n // 8
    y = (n // 2) % 4
    core = n % 2

    def net(k):
        return (n + k) & (NETS - 1)

    def away(k, way=1):
        return (((x + way * (k // 8)) & 3) * 8) + (((y + way * (k // 2 % 4)) & 3) * 2) + ((core + k) & 1)

    def dev(j):
        return (d + j) & (DEVS - 1)

    def copy(a, b, send, recv, to_net, to_dev):
        return pltpu.make_async_remote_copy(src_ref=a, dst_ref=b, send_sem=send, recv_sem=recv,
                                            device_id=(to_net, to_dev), device_id_type=MESH)

    pairs = [(state0, st), (bgain, gi), (ogain, go), (owner_i, own_v), (bus_i, bus_v), (from_i, from_v), (to_i, to_v),
             (delay_i, delay_v), (imped_i, imped_v), (fpast, fp), (tpast, tp), (source, src), (zinv, z)]
    loads = [pltpu.make_async_copy(a, b, in_s.at[i]) for i, (a, b) in enumerate(pairs)]

    def raw_copy(c):
        return pltpu.make_async_copy(prop.at[:, pl.ds(8 * c, 8), :], raw.at[c], raw_s.at[c])

    for load in loads[:3]:
        load.start()
    for c in range(16):
        raw_copy(c).start()
    for load in loads[3:]:
        load.start()

    bar = pltpu.get_barrier_semaphore()

    def greet(to_net, to_dev):
        pl.semaphore_signal(bar, inc=1, device_id=(to_net, to_dev), device_id_type=MESH)

    for g in ALL_FAR_FIRST:
        greet(away(g % NETS), dev(g // NETS))

    for load in loads[:3]:
        load.wait()
    xp[0] = st[...].T
    xb[0] = gi[...].T
    rp[0] = go[...].T
    flat = raw.reshape(16, 1024, 128)
    zero = jnp.zeros((128, 128), F32)

    def passes(i, x=None, b=None, r=None):
        def group(c, held):
            ax, ab = held
            if not i:
                raw_copy(c).wait()
            rows = []
            for kk in range(8):
                k = 8 * c + kk
                if i:
                    a = at[k]
                else:
                    a = flat[c, pl.ds(kk, 128, stride=8), :].T
                    at[k] = a
                if x is not None:
                    ax = ax + a * xp[x, pl.ds(k, 1), :]
                if b is not None:
                    ab = ab + a * xb[b, pl.ds(k, 1), :]
                if r is not None:
                    rows.append(rows_sum(a * rp[r]))
            if r is not None:
                rp[r + 1, pl.ds(8 * c, 8), :] = jnp.concatenate(rows, axis=0)
            return ax, ab

        ax, ab = lax.fori_loop(0, 16, group, (zero if x is not None else 0, zero if b is not None else 0))
        if x is not None:
            xp[x + 1] = ax
        if b is not None:
            xb[b + 1] = ab

    passes(0, x=0, b=0, r=0)

    for load in loads[3:11]:
        load.wait()
    owner = own_v[...].astype(F32)
    own_x = jnp.floor(owner * 0.125)
    own_y = jnp.floor((owner - 8.0 * own_x) * 0.5)
    own_c = owner - 8.0 * own_x - 2.0 * own_y

    def steps_to(to, at, size):
        gap = to - at.astype(F32)
        return jnp.where(gap < 0.0, gap + size, gap)

    offset = 8.0 * steps_to(own_x, x, 4.0) + 2.0 * steps_to(own_y, y, 4.0) + steps_to(own_c, core, 2.0)
    wide = jnp.broadcast_to(owner, (128, 128))
    earlier = one(wide.T == wide) * one(iota((128, 128), 0) < iota((128, 128), 1))
    rank = rows_sum(earlier)
    own = one(iota_f((NETS, 128), 0) == offset).astype(BF16)
    seat = one(iota_f((CAP, 128), 0) == rank)
    pack[0:1, :] = to_v[...].astype(F32)
    pack[1:2, :] = delay_v[...].astype(F32)
    pack[2:3, :] = imped_v[...]
    pack[3:9, :] = fp[...]
    pack[9:16, :] = jnp.zeros((7, 512), F32)

    def free_of(i, j):
        return rows_sum(xp[i] * rp[j])

    def gain_of(i, j):
        return rows_sum(xb[i] * rp[j])

    def a_copy(b, k):
        return copy(asend.at[b, k], arecv.at[b, k], a_s.at[b], a_r.at[b], away(k), d)

    def a_all(b):
        rest = pl.ds(1, NETS - 1)
        return copy(asend.at[b, rest], arecv.at[b, rest], a_s.at[b], a_r.at[b], away(1), d)

    def first_copy(g):
        return copy(asend.at[0, g % NETS], arecv0.at[g], a_s.at[0], a_r.at[0], away(g % NETS), dev(g // NETS))

    def first_all():
        rest = pl.ds(1, NETS * DEVS - 1)
        return copy(arecv0.at[rest], arecv0.at[rest], a_s.at[0], a_r.at[0], away(1), d)

    def send_batch(b, values):
        table = [value * seat for value in values]
        if len(values) < 8:
            table.append(jnp.zeros((128 - CAP * len(values), 128), F32))
        packed = sum(nt(own, piece) for piece in parts(jnp.concatenate(table, axis=0)))
        asend[b, :, 0, :] = packed
        if b:
            arecv[b, 0] = packed[0:1, :]
            for k in FAR_FIRST:
                a_copy(b, k).start()
        else:
            arecv0[0] = packed[0:1, :]
            for g in ALL_FAR_FIRST:
                first_copy(g).start()

    def v_copy(b, j):
        return copy(vall.at[b, d], vall.at[b, d], v_s.at[b, j], v_r.at[b, d], n, dev(j))

    def v_wait(b, j):
        return copy(vall.at[b, dev(j)], vall.at[b, dev(j)], v_s.at[b, j], v_r.at[b, dev(j)], n, dev(j))

    def unpack(ref, at):
        mask = one(iota((CAP, 128), 1) % CAP == iota((CAP, 128), 0))
        collect = one(iota((8, 128), 1) // CAP == iota((8, 128), 0)).astype(BF16)
        spread = jnp.concatenate([ref[at + k] * mask for k in range(NETS)], axis=0)
        return sum(nt(collect, piece) for piece in parts(spread))

    def share_batch(b):
        a_all(b).wait_recv()
        vall[b, d] = unpack(arecv.at[b], 0)
        for j in range(1, DEVS):
            v_copy(b, j).start()

    row = iota((8, 1), 0)
    row_high = ((row // 2) * 8 + 2 * d + row % 2).astype(F32)
    row32 = iota((32, 1), 0)
    high32 = (((row32 % 8) // 2) * 8 + 2 * (row32 // 8) + row32 % 2).astype(F32)
    slot_high = []

    def place_batch(b, count):
        first_rows = 8 if b else 32
        total = 0.0
        for j in range(DEVS):
            if b:
                if j:
                    v_wait(b, j).wait_recv()
                vals = vall[b, dev(j)]
                whole = brow[j]
            else:
                vals = unpack(arecv0, NETS * ((DEVS - j) % DEVS))
                bus = vals[7:8, :] - 1.0
                b_high = jnp.floor(bus * (1.0 / 128.0))
                slot_high.append(b_high)
                hots[j] = one(iota_f((128, 512), 0) == bus - 128.0 * b_high).astype(BF16)
                brow[j] = one(b_high == row_high)
                whole = one(b_high == high32)
            left = jnp.concatenate([vals[0:1, :] * whole] + [vals[q:q + 1, :] * brow[j] for q in range(1, count)], axis=0)
            total = total + nt(jnp.concatenate(parts(left), axis=0), hots[j])
        total = add_parts(total)
        return [total[:first_rows]] + [total[first_rows + 8 * q:first_rows + 8 * q + 8] for q in range(count - 1)]

    passes(1, x=1)
    pl.semaphore_wait(bar, NETS * DEVS - 1)
    line_copy = copy(pack, prev, l_s, l_r, net(1), d)
    line_copy.start()
    send_batch(0, [free_of(0, 0), free_of(1, 0), free_of(1, 1), free_of(2, 1),
                   gain_of(0, 0), gain_of(1, 0), gain_of(1, 1), bus_v[...].astype(F32) + 1.0])

    line_copy.wait_recv()
    ends = jnp.concatenate([from_v[...].astype(F32), prev[0:1, :]], axis=1)
    delay = jnp.concatenate([pack[1:2, :], prev[1:2, :]], axis=1)
    twice = 2.0 / jnp.concatenate([pack[2:3, :], prev[2:3, :]], axis=1)
    waves = [jnp.concatenate([tp[i:i + 1, :], prev[3 + i:4 + i, :]], axis=1) for i in range(DMAX)]
    high = jnp.floor(ends * (1.0 / 128.0))
    ohl[...] = one(iota_f((128, 1024), 0) == ends - 128.0 * high).astype(BF16)
    mine = rows_sum(one(high == row_high))

    def arrivals(t):
        got = jnp.zeros((1, 1024), F32)
        for lag in range(DMIN, DMAX + 1):
            if DMAX + t - lag < len(waves):
                got = jnp.where(delay == float(lag), waves[DMAX + t - lag], got)
        return got

    def inject(t):
        left = jnp.concatenate(parts(one(high == high32) * arrive[t]), axis=0)
        jl[t] = add_parts(nt(left, ohl[...])).reshape(DEVS, 8, 128)

    def sample(v):
        left = jnp.concatenate(parts(v), axis=0)
        return rows_sum(add_parts(nn(left, ohl[...])) * one(high == row_high))

    arrive = [arrivals(0), arrivals(1)]
    inject(0)
    inject(1)

    def um_copy(t, j):
        return copy(um.at[t, d], um.at[t, d], um_s.at[t], um_r.at[t, d], n, dev(j))

    def um_wait(t, j):
        return copy(um.at[t, dev(j)], um.at[t, dev(j)], um_s.at[t], um_r.at[t, dev(j)], n, dev(j))

    def um_all(t):
        sent = um.at[t, pl.ds(0, DEVS - 1)]
        return copy(sent, sent, um_s.at[t], um_r.at[t, d], n, dev(1))

    def vv_copy(half, j, sender):
        steps = pl.ds(0, STEPS - 2) if half == 0 else pl.ds(STEPS - 2, 2)
        return copy(vv.at[sender, steps], vv.at[sender, steps], vv_s.at[half, j], vv_r.at[half, sender], n, dev(j))

    def w_copy(t, way, j):
        return copy(wsend.at[t, way], wrecv.at[t, way, d], w_s.at[t], w_r.at[t], net(1 if way == 0 else NETS - 1), dev(j))

    def w_all(t):
        return copy(wrecv.at[t], wrecv.at[t], w_s.at[t], w_r.at[t], net(1), d)

    def send_waves(t):
        wave = mine * (sample(volts[t]) * twice - arrive[t])
        wsend[t, 0] = wave[:, :512]
        wsend[t, 1] = wave[:, 512:]
        for j in (2, 1, 3, 0):
            for way in range(2):
                w_copy(t, way, j).start()

    def take_waves(t):
        w_all(t).wait_recv()
        waves.append(jnp.concatenate([sum(wrecv[t, 1, j] for j in range(DEVS)),
                                      sum(wrecv[t, 0, j] for j in range(DEVS))], axis=1))
        arrive.append(arrivals(t + DMIN))
        inject(t + DMIN)

    def columns(t, c, s):
        tiles = um[t, c] + jl[t, c]
        total = None
        for e in range(2):
            lanes = pl.ds(pl.multiple_of(256 * c + 128 * e, 128), 128)
            term = z[s, :, lanes] * tiles[2 * s + e:2 * s + e + 1, :]
            total = term if total is None else total + term
        return total

    def solve(t):
        for s in range(4):
            acc[s] = columns(t, d, s)
        if t:
            um_wait(t, 1).wait_recv()
            um_wait(t, 3).wait_recv()
        for s in range(4):
            acc[s] = acc[s] + columns(t, dev(1), s) + columns(t, dev(3), s)
        if t:
            um_wait(t, 2).wait_recv()
        rows = []
        for s in range(4):
            total = acc[s] + columns(t, dev(2), s)
            rows.append(rows_sum(total[:128].T))
            rows.append(rows_sum(total[128:].T))
        return jnp.concatenate(rows, axis=0)

    def keep(t):
        for c in range(8):
            for s in range(4):
                spot = 1024 * s + 128 * c
                trace[t:t + 1, spot:spot + 128] = vv[c // 2, t, 2 * s + c % 2:2 * s + c % 2 + 1, :]

    def r_copy(b, k):
        return copy(rsend.at[b, k], rrecv.at[b, k], r_s.at[b], r_r.at[b], away(k, -1), d)

    def r_all(b):
        rest = pl.ds(1, NETS - 1)
        return copy(rsend.at[b, rest], rrecv.at[b, rest], r_s.at[b], r_r.at[b], away(1), d)

    def send_back(b, steps):
        full = jnp.concatenate([vv[c, t] for t in steps for c in range(DEVS)], axis=0)
        reached = sum(nn(piece, hots[0]) for piece in parts(full))
        pick = one(slot_high[0] == high32)
        seats = one(iota((CAP, 512), 1) % CAP == iota((CAP, 512), 0))
        home = one(iota((NETS, 512), 1) // CAP == iota((NETS, 512), 0)).astype(BF16)
        table = [rows_sum(reached[32 * i:32 * i + 32] * pick) * seats for i in range(len(steps))]
        table.append(jnp.zeros((128 - CAP * len(steps), 512), F32))
        back = sum(nt(home, piece) for piece in parts(jnp.concatenate(table, axis=0)))
        rsend[b, :, 0, :] = back
        rrecv[b, 0] = back[0:1, :]
        for k in FAR_FIRST:
            r_copy(b, k).start()

    def last_copy(g):
        return copy(lsend.at[g // NETS, g % NETS // 8], lrecv.at[g], e_s, e_r, away(g % NETS, -1), dev(g // NETS))

    def last_all():
        rest = pl.ds(1, NETS * DEVS - 1)
        return copy(lrecv.at[rest], lrecv.at[rest], e_s, e_r, away(1), d)

    def send_last(early, late):
        left = jnp.concatenate(parts(jnp.concatenate([early, late], axis=0)), axis=0)
        for j in range(DEVS):
            found = add_parts(nn(left, hots[j]))
            for i in range(2):
                line = rows_sum(found[8 * i:8 * i + 8] * brow[j])
                for g in range(4):
                    lsend[j, g, i:i + 1, :] = line[:, 128 * g:128 * g + 128]
        lrecv[0] = lsend[0, 0]
        for g in ALL_FAR_FIRST:
            last_copy(g).start()

    free, gain, volts = [], [], []
    passes(2, b=1, r=1)
    first_all().wait_recv()
    got = place_batch(0, 7)
    free += got[:4]
    gain += got[4:]
    for load in loads[11:]:
        load.wait()
    for c in range(DEVS):
        um[0, c] = jnp.concatenate([src[s, c] for s in range(4)], axis=0) + free[0][8 * c:8 * c + 8]
    base = jnp.concatenate([src[s, d] for s in range(4)], axis=0)
    for t in range(STEPS):
        if 1 <= t <= STEPS - DMIN:
            send_waves(t - 1)
        if t == 1:
            send_batch(1, [free_of(2, 2), gain_of(1, 2), gain_of(2, 2)])
            passes(3, x=2, b=2, r=2)
        if t == 2:
            passes(4, x=3)
            send_batch(2, [free_of(3, 2), free_of(3, 3), free_of(4, 3), gain_of(3, 2), gain_of(3, 3)])
        if t >= 2:
            take_waves(t - 2)
        if t == 2:
            share_batch(1)
        if t == 3:
            got = place_batch(1, 3)
            free += got[:1]
            gain += got[1:]
            passes(5, x=4)
            share_batch(2)
        if t == 4:
            passes(6, x=5)
            got = place_batch(2, 5)
            free += got[:3]
            gain += got[3:]
        if t == 5:
            passes(7, x=6, b=3)
        if t == 6:
            for j in (2, 1, 3):
                vv_copy(0, j, d).start()
            passes(8, x=7, b=4)
        if t == 7:
            for j in range(1, DEVS):
                vv_copy(0, j, dev(j)).wait_recv()
            send_back(0, list(range(STEPS - 2)))
        ready = base
        if t + 1 < STEPS:
            ready = ready + free[t + 1]
            for k in range(t):
                ready = ready + gain[t - k] * volts[k]
        v = solve(t)
        volts.append(v)
        if t + 1 < STEPS:
            um[t + 1, d] = ready + gain[0] * v
            for j in (2, 1, 3):
                um_copy(t + 1, j).start()
        vv[d, t] = v
    for j in (2, 1, 3):
        vv_copy(1, j, d).start()
    send_last(volts[-2], volts[-1])

    passes(9, b=5)
    passes(10, b=6)
    for t in range(STEPS - 2):
        keep(t)
    line_copy.wait_send()
    first_all().wait_send()
    for b in range(1, 3):
        a_all(b).wait_send()
        for j in range(1, DEVS):
            v_copy(b, j).wait_send()
    for t in range(1, STEPS):
        um_all(t).wait_send()
    for j in range(1, DEVS):
        vv_copy(0, j, d).wait_send()
        vv_copy(1, j, d).wait_send()
    for t in range(STEPS - DMIN):
        w_all(t).wait_send()
    r_all(0).wait_recv()
    by_seat = sum(tn(piece, own) for piece in parts(rrecv[0, :, 0, :]))
    state = xp[8]
    for t in range(STEPS - 2):
        state = state + rows_sum(by_seat[CAP * t:CAP * t + CAP] * seat) * xb[STEPS - 1 - t]
    state = state.T
    next_gain = xb[1].T
    spot = CAP * (offset - 8.0 * jnp.floor(offset * 0.125)) + rank
    spots = one(iota_f((128, 128), 0) == spot).T
    r_all(0).wait_send()
    for j in range(1, DEVS):
        vv_copy(1, j, dev(j)).wait_recv()
    keep(STEPS - 2)
    keep(STEPS - 1)
    last_all().wait_recv()
    columns_of = []
    for i in range(2):
        answer = sum(lrecv[NETS * j:NETS * j + NETS, i, :] for j in range(DEVS))
        by_model = sum(tn(own, piece) for piece in parts(answer))
        columns_of.append(jnp.sum(by_model * spots, axis=1, keepdims=True))
    final[...] = state + columns_of[0] * next_gain + columns_of[1] * gi[...]
    last_all().wait_send()


def body(zinv, source, model_state, propagator, input_gain, output_gain, model_owner, model_bus,
         line_from, line_to, line_delay, line_imped, wave_from_past, wave_to_past):
    vmem, dma = pltpu.VMEM, pltpu.SemaphoreType.DMA
    i32 = jnp.int32
    scratch = [
        vmem((4, 256, 1024), F32), vmem((4, DEVS, 2, 128), F32), vmem((128, 128), F32), vmem((128, 128), F32),
        vmem((128, 128), F32), vmem((1, 128), i32), vmem((1, 128), i32), vmem((1, 512), i32), vmem((1, 512), i32),
        vmem((1, 512), i32), vmem((1, 512), F32), vmem((DMAX, 512), F32), vmem((DMAX, 512), F32),
        vmem((16, 128, 8, 128), F32), vmem((128, 128, 128), F32), vmem((STEPS + 1, 128, 128), F32),
        vmem((STEPS, 128, 128), F32), vmem((4, 128, 128), F32), vmem((3, NETS, 1, 128), F32),
        vmem((3, NETS, 1, 128), F32), vmem((NETS * DEVS, 1, 128), F32), vmem((3, DEVS, 8, 512), F32), vmem((STEPS, DEVS, 8, 128), F32), vmem((DEVS, STEPS, 8, 128), F32), vmem((16, 512), F32),
        vmem((16, 512), F32), vmem((6, 2, 1, 512), F32), vmem((6, 2, DEVS, 1, 512), F32),
        vmem((1, NETS, 1, 128), F32), vmem((1, NETS, 1, 128), F32),
        vmem((DEVS, 4, 2, 128), F32), vmem((NETS * DEVS, 2, 128), F32), vmem((128, 1024), BF16),
        vmem((DEVS, 128, 512), BF16), vmem((DEVS, 8, 512), F32), vmem((4, 256, 128), F32),
        vmem((STEPS, DEVS, 8, 128), F32),
        dma((13,)), dma((16,)), dma((3,)), dma((3,)), dma((3, DEVS)), dma((3, DEVS)),
        dma((STEPS,)), dma((STEPS, DEVS)), dma((2, DEVS)), dma((2, DEVS)), dma((6,)), dma((6,)), dma, dma, dma((1,)), dma((1,)), dma, dma,
    ]
    v = pl.BlockSpec(memory_space=vmem)
    return pl.pallas_call(
        grid_kernel,
        out_shape=(vmem((STEPS, 4096), F32), vmem((128, 128), F32)),
        in_specs=[pl.BlockSpec(memory_space=pl.ANY)] * 14,
        out_specs=(v, v),
        scratch_shapes=scratch,
        compiler_params=pltpu.CompilerParams(collective_id=0, has_side_effects=True, vmem_limit_bytes=56 << 20),
    )(zinv, source.reshape(4, DEVS, 2, 128), model_state, propagator, input_gain, output_gain,
      model_owner.reshape(1, 128), model_bus.reshape(1, 128), line_from.reshape(1, 512), line_to.reshape(1, 512),
      line_delay.reshape(1, 512), line_imped.reshape(1, 512), wave_from_past, wave_to_past)


def solution(mesh):
    one_axis, both = P("net"), P(("net", "dev"))
    two = P(("net", "dev"), None)
    in_specs = (P("net", "dev", None), one_axis, two, P(("net", "dev"), None, None), two, two, two, both,
                one_axis, one_axis, one_axis, one_axis, P(None, "net"), P(None, "net"))
    return jax.shard_map(body, mesh=mesh, in_specs=in_specs, out_specs=(P(None, "net"), two), check_vma=False)
```

```python
import jax
import jax.numpy as jnp
from jax import lax
from jax.experimental import pallas as pl
from jax.experimental.pallas import tpu as pltpu
from jax.sharding import PartitionSpec as P

STEPS = 8
DMIN = 2
DMAX = 6
NETS = 32
DEVS = 4
CAP = 16
PARTS = 2
F32 = jnp.float32
BF16 = jnp.bfloat16
MESH = pl.DeviceIdType.MESH


def rows_sum(x):
    return jnp.sum(x, axis=0, keepdims=True)


def parts(x, count=PARTS):
    pieces = []
    for i in range(count):
        piece = x.astype(BF16)
        pieces.append(piece)
        if i + 1 < count:
            x = x - piece.astype(F32)
    return pieces


def dot(a, b, dims):
    return lax.dot_general(a, b, (dims, ((), ())), preferred_element_type=F32)


def nn(a, b):
    return dot(a, b, ((1,), (0,)))


def nt(a, b):
    return dot(a, b, ((1,), (1,)))


def tn(a, b):
    return dot(a, b, ((0,), (0,)))


def iota(shape, dim):
    return lax.broadcasted_iota(jnp.int32, shape, dim)


def iota_f(shape, dim):
    return iota(shape, dim).astype(F32)


def one(mask):
    return jnp.where(mask, 1.0, 0.0).astype(F32)


def add_parts(x):
    rows = x.shape[0] // PARTS
    return sum(x[rows * i:rows * i + rows] for i in range(PARTS))


def hops(k):
    x, y, z = (min(v, 4 - v) for v in (k // 8 % 4, k // 2 % 4, k // 32))
    return x + y + z + k % 2 * 0.5


FAR_FIRST = sorted(range(1, NETS), key=hops, reverse=True)
ALL_FAR_FIRST = sorted(range(1, NETS * DEVS), key=hops, reverse=True)


def grid_kernel(zinv, source, state0, prop, bgain, ogain, owner_i, bus_i, from_i, to_i, delay_i, imped_i, fpast, tpast,
                trace, final,
                z, src, st, gi, go, own_v, bus_v, from_v, to_v, delay_v, imped_v, fp, tp,
                raw, at, xp, xb, rp, asend, arecv, arecv0, vall, um, vv, pack, prev, wsend, wrecv, rsend, rrecv, lsend, lrecv,
                ohl, hots, brow, acc, jl,
                in_s, raw_s, a_s, a_r, v_s, v_r, um_s, um_r, vv_s, vv_r, w_s, w_r, l_s, l_r, r_s, r_r, e_s, e_r):
    n = lax.axis_index("net")
    d = lax.axis_index("dev")

    x = n // 8
    y = (n // 2) % 4
    core = n % 2

    def net(k):
        return (n + k) & (NETS - 1)

    def away(k, way=1):
        return (((x + way * (k // 8)) & 3) * 8) + (((y + way * (k // 2 % 4)) & 3) * 2) + ((core + k) & 1)

    def dev(j):
        return (d + j) & (DEVS - 1)

    def copy(a, b, send, recv, to_net, to_dev):
        return pltpu.make_async_remote_copy(src_ref=a, dst_ref=b, send_sem=send, recv_sem=recv,
                                            device_id=(to_net, to_dev), device_id_type=MESH)

    pairs = [(state0, st), (bgain, gi), (ogain, go), (owner_i, own_v), (bus_i, bus_v), (from_i, from_v), (to_i, to_v),
             (delay_i, delay_v), (imped_i, imped_v), (fpast, fp), (tpast, tp), (source, src), (zinv, z)]
    loads = [pltpu.make_async_copy(a, b, in_s.at[i]) for i, (a, b) in enumerate(pairs)]

    def raw_copy(c):
        return pltpu.make_async_copy(prop.at[:, pl.ds(8 * c, 8), :], raw.at[c], raw_s.at[c])

    for load in loads[:3]:
        load.start()
    for c in range(16):
        raw_copy(c).start()
    for load in loads[3:]:
        load.start()

    bar = pltpu.get_barrier_semaphore()

    def greet(to_net, to_dev):
        pl.semaphore_signal(bar, inc=1, device_id=(to_net, to_dev), device_id_type=MESH)

    for g in ALL_FAR_FIRST:
        greet(away(g % NETS), dev(g // NETS))

    for load in loads[:3]:
        load.wait()
    xp[0] = st[...].T
    xb[0] = gi[...].T
    rp[0] = go[...].T
    flat = raw.reshape(16, 1024, 128)
    zero = jnp.zeros((128, 128), F32)

    def passes(i, x=None, b=None, r=None):
        def group(c, held):
            ax, ab = held
            if not i:
                raw_copy(c).wait()
            rows = []
            for kk in range(8):
                k = 8 * c + kk
                if i:
                    a = at[k]
                else:
                    a = flat[c, pl.ds(kk, 128, stride=8), :].T
                    at[k] = a
                if x is not None:
                    ax = ax + a * xp[x, pl.ds(k, 1), :]
                if b is not None:
                    ab = ab + a * xb[b, pl.ds(k, 1), :]
                if r is not None:
                    rows.append(rows_sum(a * rp[r]))
            if r is not None:
                rp[r + 1, pl.ds(8 * c, 8), :] = jnp.concatenate(rows, axis=0)
            return ax, ab

        ax, ab = lax.fori_loop(0, 16, group, (zero if x is not None else 0, zero if b is not None else 0))
        if x is not None:
            xp[x + 1] = ax
        if b is not None:
            xb[b + 1] = ab

    passes(0, x=0, b=0, r=0)

    for load in loads[3:11]:
        load.wait()
    owner = own_v[...].astype(F32)
    own_x = jnp.floor(owner * 0.125)
    own_y = jnp.floor((owner - 8.0 * own_x) * 0.5)
    own_c = owner - 8.0 * own_x - 2.0 * own_y

    def steps_to(to, at, size):
        gap = to - at.astype(F32)
        return jnp.where(gap < 0.0, gap + size, gap)

    offset = 8.0 * steps_to(own_x, x, 4.0) + 2.0 * steps_to(own_y, y, 4.0) + steps_to(own_c, core, 2.0)
    wide = jnp.broadcast_to(owner, (128, 128))
    earlier = one(wide.T == wide) * one(iota((128, 128), 0) < iota((128, 128), 1))
    rank = rows_sum(earlier)
    own = one(iota_f((NETS, 128), 0) == offset).astype(BF16)
    seat = one(iota_f((CAP, 128), 0) == rank)
    pack[0:1, :] = to_v[...].astype(F32)
    pack[1:2, :] = delay_v[...].astype(F32)
    pack[2:3, :] = imped_v[...]
    pack[3:9, :] = fp[...]
    pack[9:16, :] = jnp.zeros((7, 512), F32)

    def free_of(i, j):
        return rows_sum(xp[i] * rp[j])

    def gain_of(i, j):
        return rows_sum(xb[i] * rp[j])

    def a_copy(b, k):
        return copy(asend.at[b, k], arecv.at[b, k], a_s.at[b], a_r.at[b], away(k), d)

    def a_all(b):
        rest = pl.ds(1, NETS - 1)
        return copy(asend.at[b, rest], arecv.at[b, rest], a_s.at[b], a_r.at[b], away(1), d)

    def first_copy(g):
        return copy(asend.at[0, g % NETS], arecv0.at[g], a_s.at[0], a_r.at[0], away(g % NETS), dev(g // NETS))

    def first_all():
        rest = pl.ds(1, NETS * DEVS - 1)
        return copy(arecv0.at[rest], arecv0.at[rest], a_s.at[0], a_r.at[0], away(1), d)

    def send_batch(b, values):
        table = [value * seat for value in values]
        if len(values) < 8:
            table.append(jnp.zeros((128 - CAP * len(values), 128), F32))
        packed = sum(nt(own, piece) for piece in parts(jnp.concatenate(table, axis=0)))
        asend[b, :, 0, :] = packed
        if b:
            arecv[b, 0] = packed[0:1, :]
            for k in FAR_FIRST:
                a_copy(b, k).start()
        else:
            arecv0[0] = packed[0:1, :]
            for g in ALL_FAR_FIRST:
                first_copy(g).start()

    def v_copy(b, j):
        return copy(vall.at[b, d], vall.at[b, d], v_s.at[b, j], v_r.at[b, d], n, dev(j))

    def v_wait(b, j):
        return copy(vall.at[b, dev(j)], vall.at[b, dev(j)], v_s.at[b, j], v_r.at[b, dev(j)], n, dev(j))

    def unpack(ref, at):
        mask = one(iota((CAP, 128), 1) % CAP == iota((CAP, 128), 0))
        collect = one(iota((8, 128), 1) // CAP == iota((8, 128), 0)).astype(BF16)
        spread = jnp.concatenate([ref[at + k] * mask for k in range(NETS)], axis=0)
        return sum(nt(collect, piece) for piece in parts(spread))

    def share_batch(b):
        a_all(b).wait_recv()
        vall[b, d] = unpack(arecv.at[b], 0)
        for j in range(1, DEVS):
            v_copy(b, j).start()

    row = iota((8, 1), 0)
    row_high = ((row // 2) * 8 + 2 * d + row % 2).astype(F32)
    row32 = iota((32, 1), 0)
    high32 = (((row32 % 8) // 2) * 8 + 2 * (row32 // 8) + row32 % 2).astype(F32)
    slot_high = []

    def place_batch(b, count):
        first_rows = 8 if b else 32
        total = 0.0
        for j in range(DEVS):
            if b:
                if j:
                    v_wait(b, j).wait_recv()
                vals = vall[b, dev(j)]
                whole = brow[j]
            else:
                vals = unpack(arecv0, NETS * ((DEVS - j) % DEVS))
                bus = vals[7:8, :] - 1.0
                b_high = jnp.floor(bus * (1.0 / 128.0))
                slot_high.append(b_high)
                hots[j] = one(iota_f((128, 512), 0) == bus - 128.0 * b_high).astype(BF16)
                brow[j] = one(b_high == row_high)
                whole = one(b_high == high32)
            left = jnp.concatenate([vals[0:1, :] * whole] + [vals[q:q + 1, :] * brow[j] for q in range(1, count)], axis=0)
            total = total + nt(jnp.concatenate(parts(left), axis=0), hots[j])
        total = add_parts(total)
        return [total[:first_rows]] + [total[first_rows + 8 * q:first_rows + 8 * q + 8] for q in range(count - 1)]

    passes(1, x=1)
    pl.semaphore_wait(bar, NETS * DEVS - 1)
    line_copy = copy(pack, prev, l_s, l_r, net(1), d)
    line_copy.start()
    send_batch(0, [free_of(0, 0), free_of(1, 0), free_of(1, 1), free_of(2, 1),
                   gain_of(0, 0), gain_of(1, 0), gain_of(1, 1), bus_v[...].astype(F32) + 1.0])

    line_copy.wait_recv()
    ends = jnp.concatenate([from_v[...].astype(F32), prev[0:1, :]], axis=1)
    delay = jnp.concatenate([pack[1:2, :], prev[1:2, :]], axis=1)
    twice = 2.0 / jnp.concatenate([pack[2:3, :], prev[2:3, :]], axis=1)
    waves = [jnp.concatenate([tp[i:i + 1, :], prev[3 + i:4 + i, :]], axis=1) for i in range(DMAX)]
    high = jnp.floor(ends * (1.0 / 128.0))
    ohl[...] = one(iota_f((128, 1024), 0) == ends - 128.0 * high).astype(BF16)
    mine = rows_sum(one(high == row_high))

    def arrivals(t):
        got = jnp.zeros((1, 1024), F32)
        for lag in range(DMIN, DMAX + 1):
            if DMAX + t - lag < len(waves):
                got = jnp.where(delay == float(lag), waves[DMAX + t - lag], got)
        return got

    def inject(t):
        left = jnp.concatenate(parts(one(high == high32) * arrive[t]), axis=0)
        jl[t] = add_parts(nt(left, ohl[...])).reshape(DEVS, 8, 128)

    def sample(v):
        left = jnp.concatenate(parts(v), axis=0)
        return rows_sum(add_parts(nn(left, ohl[...])) * one(high == row_high))

    arrive = [arrivals(0), arrivals(1)]
    inject(0)
    inject(1)

    def um_copy(t, j):
        return copy(um.at[t, d], um.at[t, d], um_s.at[t], um_r.at[t, d], n, dev(j))

    def um_wait(t, j):
        return copy(um.at[t, dev(j)], um.at[t, dev(j)], um_s.at[t], um_r.at[t, dev(j)], n, dev(j))

    def um_all(t):
        sent = um.at[t, pl.ds(0, DEVS - 1)]
        return copy(sent, sent, um_s.at[t], um_r.at[t, d], n, dev(1))

    def vv_copy(half, j, sender):
        steps = pl.ds(0, STEPS - 2) if half == 0 else pl.ds(STEPS - 2, 2)
        return copy(vv.at[sender, steps], vv.at[sender, steps], vv_s.at[half, j], vv_r.at[half, sender], n, dev(j))

    def w_copy(t, way, j):
        return copy(wsend.at[t, way], wrecv.at[t, way, d], w_s.at[t], w_r.at[t], net(1 if way == 0 else NETS - 1), dev(j))

    def w_all(t):
        return copy(wrecv.at[t], wrecv.at[t], w_s.at[t], w_r.at[t], net(1), d)

    def send_waves(t):
        wave = mine * (sample(volts[t]) * twice - arrive[t])
        wsend[t, 0] = wave[:, :512]
        wsend[t, 1] = wave[:, 512:]
        for j in (2, 1, 3, 0):
            for way in range(2):
                w_copy(t, way, j).start()

    def take_waves(t):
        w_all(t).wait_recv()
        waves.append(jnp.concatenate([sum(wrecv[t, 1, j] for j in range(DEVS)),
                                      sum(wrecv[t, 0, j] for j in range(DEVS))], axis=1))
        arrive.append(arrivals(t + DMIN))
        inject(t + DMIN)

    def columns(t, c, s):
        tiles = um[t, c] + jl[t, c]
        total = None
        for e in range(2):
            lanes = pl.ds(pl.multiple_of(256 * c + 128 * e, 128), 128)
            term = z[s, :, lanes] * tiles[2 * s + e:2 * s + e + 1, :]
            total = term if total is None else total + term
        return total

    def solve(t):
        for s in range(4):
            acc[s] = columns(t, d, s)
        if t:
            um_wait(t, 1).wait_recv()
            um_wait(t, 3).wait_recv()
        for s in range(4):
            acc[s] = acc[s] + columns(t, dev(1), s) + columns(t, dev(3), s)
        if t:
            um_wait(t, 2).wait_recv()
        rows = []
        for s in range(4):
            total = acc[s] + columns(t, dev(2), s)
            rows.append(rows_sum(total[:128].T))
            rows.append(rows_sum(total[128:].T))
        return jnp.concatenate(rows, axis=0)

    def keep(t):
        for c in range(8):
            for s in range(4):
                spot = 1024 * s + 128 * c
                trace[t:t + 1, spot:spot + 128] = vv[c // 2, t, 2 * s + c % 2:2 * s + c % 2 + 1, :]

    def r_copy(b, k):
        return copy(rsend.at[b, k], rrecv.at[b, k], r_s.at[b], r_r.at[b], away(k, -1), d)

    def r_all(b):
        rest = pl.ds(1, NETS - 1)
        return copy(rsend.at[b, rest], rrecv.at[b, rest], r_s.at[b], r_r.at[b], away(1), d)

    def send_back(b, steps):
        full = jnp.concatenate([vv[c, t] for t in steps for c in range(DEVS)], axis=0)
        reached = sum(nn(piece, hots[0]) for piece in parts(full))
        pick = one(slot_high[0] == high32)
        seats = one(iota((CAP, 512), 1) % CAP == iota((CAP, 512), 0))
        home = one(iota((NETS, 512), 1) // CAP == iota((NETS, 512), 0)).astype(BF16)
        table = [rows_sum(reached[32 * i:32 * i + 32] * pick) * seats for i in range(len(steps))]
        table.append(jnp.zeros((128 - CAP * len(steps), 512), F32))
        back = sum(nt(home, piece) for piece in parts(jnp.concatenate(table, axis=0)))
        rsend[b, :, 0, :] = back
        rrecv[b, 0] = back[0:1, :]
        for k in FAR_FIRST:
            r_copy(b, k).start()

    def last_copy(g):
        return copy(lsend.at[g // NETS, g % NETS // 8], lrecv.at[g], e_s, e_r, away(g % NETS, -1), dev(g // NETS))

    def last_all():
        rest = pl.ds(1, NETS * DEVS - 1)
        return copy(lrecv.at[rest], lrecv.at[rest], e_s, e_r, away(1), d)

    def send_last(early, late):
        left = jnp.concatenate(parts(jnp.concatenate([early, late], axis=0)), axis=0)
        for j in range(DEVS):
            found = add_parts(nn(left, hots[j]))
            for i in range(2):
                line = rows_sum(found[8 * i:8 * i + 8] * brow[j])
                for g in range(4):
                    lsend[j, g, i:i + 1, :] = line[:, 128 * g:128 * g + 128]
        lrecv[0] = lsend[0, 0]
        for g in ALL_FAR_FIRST:
            last_copy(g).start()

    free, gain, volts = [], [], []
    passes(2, b=1, r=1)
    first_all().wait_recv()
    got = place_batch(0, 7)
    free += got[:4]
    gain += got[4:]
    for load in loads[11:]:
        load.wait()
    for c in range(DEVS):
        um[0, c] = jnp.concatenate([src[s, c] for s in range(4)], axis=0) + free[0][8 * c:8 * c + 8]
    base = jnp.concatenate([src[s, d] for s in range(4)], axis=0)
    for t in range(STEPS):
        if 1 <= t <= STEPS - DMIN:
            send_waves(t - 1)
        if t == 1:
            send_batch(1, [free_of(2, 2), gain_of(1, 2), gain_of(2, 2)])
            passes(3, x=2, b=2, r=2)
        if t == 2:
            passes(4, x=3)
            send_batch(2, [free_of(3, 2), free_of(3, 3), free_of(4, 3), gain_of(3, 2), gain_of(3, 3)])
        if t >= 2:
            take_waves(t - 2)
        if t == 2:
            share_batch(1)
        if t == 3:
            got = place_batch(1, 3)
            free += got[:1]
            gain += got[1:]
            passes(5, x=4)
            share_batch(2)
        if t == 4:
            passes(6, x=5)
            got = place_batch(2, 5)
            free += got[:3]
            gain += got[3:]
        if t == 5:
            passes(7, x=6, b=3)
        if t == 6:
            for j in (2, 1, 3):
                vv_copy(0, j, d).start()
            passes(8, x=7, b=4)
        if t == 7:
            for j in range(1, DEVS):
                vv_copy(0, j, dev(j)).wait_recv()
            send_back(0, list(range(STEPS - 2)))
        ready = base
        if t + 1 < STEPS:
            ready = ready + free[t + 1]
            for k in range(t):
                ready = ready + gain[t - k] * volts[k]
        v = solve(t)
        volts.append(v)
        if t + 1 < STEPS:
            um[t + 1, d] = ready + gain[0] * v
            for j in (2, 1, 3):
                um_copy(t + 1, j).start()
        vv[d, t] = v
    for j in (2, 1, 3):
        vv_copy(1, j, d).start()
    send_last(volts[-2], volts[-1])

    passes(9, b=5)
    passes(10, b=6)
    for t in range(STEPS - 2):
        keep(t)
    line_copy.wait_send()
    first_all().wait_send()
    for b in range(1, 3):
        a_all(b).wait_send()
        for j in range(1, DEVS):
            v_copy(b, j).wait_send()
    for t in range(1, STEPS):
        um_all(t).wait_send()
    for j in range(1, DEVS):
        vv_copy(0, j, d).wait_send()
        vv_copy(1, j, d).wait_send()
    for t in range(STEPS - DMIN):
        w_all(t).wait_send()
    r_all(0).wait_recv()
    by_seat = sum(tn(piece, own) for piece in parts(rrecv[0, :, 0, :]))
    state = xp[8]
    for t in range(STEPS - 2):
        state = state + rows_sum(by_seat[CAP * t:CAP * t + CAP] * seat) * xb[STEPS - 1 - t]
    state = state.T
    next_gain = xb[1].T
    spot = CAP * (offset - 8.0 * jnp.floor(offset * 0.125)) + rank
    spots = one(iota_f((128, 128), 0) == spot).T
    r_all(0).wait_send()
    for j in range(1, DEVS):
        vv_copy(1, j, dev(j)).wait_recv()
    keep(STEPS - 2)
    keep(STEPS - 1)
    last_all().wait_recv()
    columns_of = []
    for i in range(2):
        answer = sum(lrecv[NETS * j:NETS * j + NETS, i, :] for j in range(DEVS))
        by_model = sum(tn(own, piece) for piece in parts(answer))
        columns_of.append(jnp.sum(by_model * spots, axis=1, keepdims=True))
    final[...] = state + columns_of[0] * next_gain + columns_of[1] * gi[...]
    last_all().wait_send()


def hand_out(trace, final, trace_out, final_out, sems):
    copies = [pltpu.make_async_copy(trace, trace_out, sems.at[0]), pltpu.make_async_copy(final, final_out, sems.at[1])]
    for one_copy in copies:
        one_copy.start()
    for one_copy in copies:
        one_copy.wait()


def body(zinv, source, model_state, propagator, input_gain, output_gain, model_owner, model_bus,
         line_from, line_to, line_delay, line_imped, wave_from_past, wave_to_past):
    vmem, dma = pltpu.VMEM, pltpu.SemaphoreType.DMA
    i32 = jnp.int32
    scratch = [
        vmem((4, 256, 1024), F32), vmem((4, DEVS, 2, 128), F32), vmem((128, 128), F32), vmem((128, 128), F32),
        vmem((128, 128), F32), vmem((1, 128), i32), vmem((1, 128), i32), vmem((1, 512), i32), vmem((1, 512), i32),
        vmem((1, 512), i32), vmem((1, 512), F32), vmem((DMAX, 512), F32), vmem((DMAX, 512), F32),
        vmem((16, 128, 8, 128), F32), vmem((128, 128, 128), F32), vmem((STEPS + 1, 128, 128), F32),
        vmem((STEPS, 128, 128), F32), vmem((4, 128, 128), F32), vmem((3, NETS, 1, 128), F32),
        vmem((3, NETS, 1, 128), F32), vmem((NETS * DEVS, 1, 128), F32), vmem((3, DEVS, 8, 512), F32), vmem((STEPS, DEVS, 8, 128), F32), vmem((DEVS, STEPS, 8, 128), F32), vmem((16, 512), F32),
        vmem((16, 512), F32), vmem((6, 2, 1, 512), F32), vmem((6, 2, DEVS, 1, 512), F32),
        vmem((1, NETS, 1, 128), F32), vmem((1, NETS, 1, 128), F32),
        vmem((DEVS, 4, 2, 128), F32), vmem((NETS * DEVS, 2, 128), F32), vmem((128, 1024), BF16),
        vmem((DEVS, 128, 512), BF16), vmem((DEVS, 8, 512), F32), vmem((4, 256, 128), F32),
        vmem((STEPS, DEVS, 8, 128), F32),
        dma((13,)), dma((16,)), dma((3,)), dma((3,)), dma((3, DEVS)), dma((3, DEVS)),
        dma((STEPS,)), dma((STEPS, DEVS)), dma((2, DEVS)), dma((2, DEVS)), dma((6,)), dma((6,)), dma, dma, dma((1,)), dma((1,)), dma, dma,
    ]
    v = pl.BlockSpec(memory_space=vmem)
    found = pl.pallas_call(
        grid_kernel,
        out_shape=(vmem((STEPS, 4096), F32), vmem((128, 128), F32)),
        in_specs=[pl.BlockSpec(memory_space=pl.ANY)] * 14,
        out_specs=(v, v),
        scratch_shapes=scratch,
        compiler_params=pltpu.CompilerParams(collective_id=0, has_side_effects=True, vmem_limit_bytes=56 << 20),
    )(zinv, source.reshape(4, DEVS, 2, 128), model_state, propagator, input_gain, output_gain,
      model_owner.reshape(1, 128), model_bus.reshape(1, 128), line_from.reshape(1, 512), line_to.reshape(1, 512),
      line_delay.reshape(1, 512), line_imped.reshape(1, 512), wave_from_past, wave_to_past)
    return pl.pallas_call(
        hand_out,
        out_shape=(jax.ShapeDtypeStruct((STEPS, 4096), F32), jax.ShapeDtypeStruct((128, 128), F32)),
        in_specs=[v, v],
        out_specs=(pl.BlockSpec(memory_space=pl.ANY), pl.BlockSpec(memory_space=pl.ANY)),
        scratch_shapes=[dma((2,))],
        compiler_params=pltpu.CompilerParams(vmem_limit_bytes=40 << 20),
    )(*found)


def solution(mesh):
    one_axis, both = P("net"), P(("net", "dev"))
    two = P(("net", "dev"), None)
    in_specs = (P("net", "dev", None), one_axis, two, P(("net", "dev"), None, None), two, two, two, both,
                one_axis, one_axis, one_axis, one_axis, P(None, "net"), P(None, "net"))
    return jax.shard_map(body, mesh=mesh, in_specs=in_specs, out_specs=(P(None, "net"), two), check_vma=False)
```

```python
import jax
import jax.numpy as jnp
from jax import lax
from jax.experimental import pallas as pl
from jax.experimental.pallas import tpu as pltpu
from jax.sharding import PartitionSpec as P

STEPS = 8
DMIN = 2
DMAX = 6
NETS = 32
DEVS = 4
CAP = 16
PARTS = 2
F32 = jnp.float32
BF16 = jnp.bfloat16
MESH = pl.DeviceIdType.MESH


def rows_sum(x):
    return jnp.sum(x, axis=0, keepdims=True)


def parts(x, count=PARTS):
    pieces = []
    for i in range(count):
        piece = x.astype(BF16)
        pieces.append(piece)
        if i + 1 < count:
            x = x - piece.astype(F32)
    return pieces


def dot(a, b, dims):
    return lax.dot_general(a, b, (dims, ((), ())), preferred_element_type=F32)


def nn(a, b):
    return dot(a, b, ((1,), (0,)))


def nt(a, b):
    return dot(a, b, ((1,), (1,)))


def tn(a, b):
    return dot(a, b, ((0,), (0,)))


def iota(shape, dim):
    return lax.broadcasted_iota(jnp.int32, shape, dim)


def iota_f(shape, dim):
    return iota(shape, dim).astype(F32)


def one(mask):
    return jnp.where(mask, 1.0, 0.0).astype(F32)


def add_parts(x):
    rows = x.shape[0] // PARTS
    return sum(x[rows * i:rows * i + rows] for i in range(PARTS))


def hops(k):
    x, y, z = (min(v, 4 - v) for v in (k // 8 % 4, k // 2 % 4, k // 32))
    return x + y + z + k % 2 * 0.5


FAR_FIRST = sorted(range(1, NETS), key=hops, reverse=True)
ALL_FAR_FIRST = sorted(range(1, NETS * DEVS), key=hops, reverse=True)


def grid_kernel(zinv, source, state0, prop, bgain, ogain, owner_i, bus_i, from_i, to_i, delay_i, imped_i, fpast, tpast,
                trace, final,
                z, src, st, gi, go, own_v, bus_v, from_v, to_v, delay_v, imped_v, fp, tp,
                raw, at, xp, xb, rp, asend, arecv, arecv0, vall, um, vv, pack, prev, wsend, wrecv, rsend, rrecv, lsend, lrecv,
                ohl, hots, brow, acc, jl,
                in_s, raw_s, a_s, a_r, v_s, v_r, um_s, um_r, vv_s, vv_r, w_s, w_r, l_s, l_r, r_s, r_r, e_s, e_r):
    n = lax.axis_index("net")
    d = lax.axis_index("dev")

    x = n // 8
    y = (n // 2) % 4
    core = n % 2

    def net(k):
        return (n + k) & (NETS - 1)

    def away(k, way=1):
        return (((x + way * (k // 8)) & 3) * 8) + (((y + way * (k // 2 % 4)) & 3) * 2) + ((core + k) & 1)

    def dev(j):
        return (d + j) & (DEVS - 1)

    def copy(a, b, send, recv, to_net, to_dev):
        return pltpu.make_async_remote_copy(src_ref=a, dst_ref=b, send_sem=send, recv_sem=recv,
                                            device_id=(to_net, to_dev), device_id_type=MESH)

    pairs = [(state0, st), (bgain, gi), (ogain, go), (owner_i, own_v), (bus_i, bus_v), (from_i, from_v), (to_i, to_v),
             (delay_i, delay_v), (imped_i, imped_v), (fpast, fp), (tpast, tp), (source, src), (zinv, z)]
    loads = [pltpu.make_async_copy(a, b, in_s.at[i]) for i, (a, b) in enumerate(pairs)]

    def raw_copy(c):
        return pltpu.make_async_copy(prop.at[:, pl.ds(8 * c, 8), :], raw.at[c], raw_s.at[c])

    for load in loads[:3]:
        load.start()
    for c in range(16):
        raw_copy(c).start()
    for load in loads[3:]:
        load.start()

    bar = pltpu.get_barrier_semaphore()

    def greet(to_net, to_dev):
        pl.semaphore_signal(bar, inc=1, device_id=(to_net, to_dev), device_id_type=MESH)

    for g in ALL_FAR_FIRST:
        greet(away(g % NETS), dev(g // NETS))

    for load in loads[:3]:
        load.wait()
    xp[0] = st[...].T
    xb[0] = gi[...].T
    rp[0] = go[...].T
    flat = raw.reshape(16, 1024, 128)
    zero = jnp.zeros((128, 128), F32)

    def passes(i, x=None, b=None, r=None):
        def group(c, held):
            ax, ab = held
            if not i:
                raw_copy(c).wait()
            rows = []
            for kk in range(8):
                k = 8 * c + kk
                if i:
                    a = at[k]
                else:
                    a = flat[c, pl.ds(kk, 128, stride=8), :].T
                    at[k] = a
                if x is not None:
                    ax = ax + a * xp[x, pl.ds(k, 1), :]
                if b is not None:
                    ab = ab + a * xb[b, pl.ds(k, 1), :]
                if r is not None:
                    rows.append(rows_sum(a * rp[r]))
            if r is not None:
                rp[r + 1, pl.ds(8 * c, 8), :] = jnp.concatenate(rows, axis=0)
            return ax, ab

        ax, ab = lax.fori_loop(0, 16, group, (zero if x is not None else 0, zero if b is not None else 0))
        if x is not None:
            xp[x + 1] = ax
        if b is not None:
            xb[b + 1] = ab

    passes(0, x=0, b=0, r=0)

    for load in loads[3:11]:
        load.wait()
    owner = own_v[...].astype(F32)
    own_x = jnp.floor(owner * 0.125)
    own_y = jnp.floor((owner - 8.0 * own_x) * 0.5)
    own_c = owner - 8.0 * own_x - 2.0 * own_y

    def steps_to(to, at, size):
        gap = to - at.astype(F32)
        return jnp.where(gap < 0.0, gap + size, gap)

    offset = 8.0 * steps_to(own_x, x, 4.0) + 2.0 * steps_to(own_y, y, 4.0) + steps_to(own_c, core, 2.0)
    wide = jnp.broadcast_to(owner, (128, 128))
    earlier = one(wide.T == wide) * one(iota((128, 128), 0) < iota((128, 128), 1))
    rank = rows_sum(earlier)
    own = one(iota_f((NETS, 128), 0) == offset).astype(BF16)
    seat = one(iota_f((CAP, 128), 0) == rank)
    pack[0:1, :] = to_v[...].astype(F32)
    pack[1:2, :] = delay_v[...].astype(F32)
    pack[2:3, :] = imped_v[...]
    pack[3:9, :] = fp[...]
    pack[9:16, :] = jnp.zeros((7, 512), F32)

    def free_of(i, j):
        return rows_sum(xp[i] * rp[j])

    def gain_of(i, j):
        return rows_sum(xb[i] * rp[j])

    def a_copy(b, k):
        return copy(asend.at[b, k], arecv.at[b, k], a_s.at[b], a_r.at[b], away(k), d)

    def a_all(b):
        rest = pl.ds(1, NETS - 1)
        return copy(asend.at[b, rest], arecv.at[b, rest], a_s.at[b], a_r.at[b], away(1), d)

    def first_copy(g):
        return copy(asend.at[0, g % NETS], arecv0.at[g], a_s.at[0], a_r.at[0], away(g % NETS), dev(g // NETS))

    def first_all():
        rest = pl.ds(1, NETS * DEVS - 1)
        return copy(arecv0.at[rest], arecv0.at[rest], a_s.at[0], a_r.at[0], away(1), d)

    def send_batch(b, values):
        table = [value * seat for value in values]
        if len(values) < 8:
            table.append(jnp.zeros((128 - CAP * len(values), 128), F32))
        packed = sum(nt(own, piece) for piece in parts(jnp.concatenate(table, axis=0)))
        asend[b, :, 0, :] = packed
        if b:
            arecv[b, 0] = packed[0:1, :]
            for k in FAR_FIRST:
                a_copy(b, k).start()
        else:
            arecv0[0] = packed[0:1, :]
            for g in ALL_FAR_FIRST:
                first_copy(g).start()

    def v_copy(b, j):
        return copy(vall.at[b, d], vall.at[b, d], v_s.at[b, j], v_r.at[b, d], n, dev(j))

    def v_wait(b, j):
        return copy(vall.at[b, dev(j)], vall.at[b, dev(j)], v_s.at[b, j], v_r.at[b, dev(j)], n, dev(j))

    def unpack(ref, at):
        mask = one(iota((CAP, 128), 1) % CAP == iota((CAP, 128), 0))
        collect = one(iota((8, 128), 1) // CAP == iota((8, 128), 0)).astype(BF16)
        spread = jnp.concatenate([ref[at + k] * mask for k in range(NETS)], axis=0)
        return sum(nt(collect, piece) for piece in parts(spread))

    def share_batch(b):
        a_all(b).wait_recv()
        vall[b, d] = unpack(arecv.at[b], 0)
        for j in range(1, DEVS):
            v_copy(b, j).start()

    row = iota((8, 1), 0)
    row_high = ((row // 2) * 8 + 2 * d + row % 2).astype(F32)
    row32 = iota((32, 1), 0)
    high32 = (((row32 % 8) // 2) * 8 + 2 * (row32 // 8) + row32 % 2).astype(F32)
    slot_high = []

    def place_batch(b, count):
        first_rows = 8 if b else 32
        total = 0.0
        for j in range(DEVS):
            if b:
                if j:
                    v_wait(b, j).wait_recv()
                vals = vall[b, dev(j)]
                whole = brow[j]
            else:
                vals = unpack(arecv0, NETS * ((DEVS - j) % DEVS))
                bus = vals[7:8, :] - 1.0
                b_high = jnp.floor(bus * (1.0 / 128.0))
                slot_high.append(b_high)
                hots[j] = one(iota_f((128, 512), 0) == bus - 128.0 * b_high).astype(BF16)
                brow[j] = one(b_high == row_high)
                whole = one(b_high == high32)
            left = jnp.concatenate([vals[0:1, :] * whole] + [vals[q:q + 1, :] * brow[j] for q in range(1, count)], axis=0)
            total = total + nt(jnp.concatenate(parts(left), axis=0), hots[j])
        total = add_parts(total)
        return [total[:first_rows]] + [total[first_rows + 8 * q:first_rows + 8 * q + 8] for q in range(count - 1)]

    passes(1, x=1)
    pl.semaphore_wait(bar, NETS * DEVS - 1)
    line_copy = copy(pack, prev, l_s, l_r, net(1), d)
    line_copy.start()
    send_batch(0, [free_of(0, 0), free_of(1, 0), free_of(1, 1), free_of(2, 1),
                   gain_of(0, 0), gain_of(1, 0), gain_of(1, 1), bus_v[...].astype(F32) + 1.0])

    line_copy.wait_recv()
    ends = jnp.concatenate([from_v[...].astype(F32), prev[0:1, :]], axis=1)
    delay = jnp.concatenate([pack[1:2, :], prev[1:2, :]], axis=1)
    twice = 2.0 / jnp.concatenate([pack[2:3, :], prev[2:3, :]], axis=1)
    waves = [jnp.concatenate([tp[i:i + 1, :], prev[3 + i:4 + i, :]], axis=1) for i in range(DMAX)]
    high = jnp.floor(ends * (1.0 / 128.0))
    ohl[...] = one(iota_f((128, 1024), 0) == ends - 128.0 * high).astype(BF16)
    mine = rows_sum(one(high == row_high))

    def arrivals(t):
        got = jnp.zeros((1, 1024), F32)
        for lag in range(DMIN, DMAX + 1):
            if DMAX + t - lag < len(waves):
                got = jnp.where(delay == float(lag), waves[DMAX + t - lag], got)
        return got

    def inject(t):
        left = jnp.concatenate(parts(one(high == high32) * arrive[t]), axis=0)
        jl[t] = add_parts(nt(left, ohl[...])).reshape(DEVS, 8, 128)

    def sample(v):
        left = jnp.concatenate(parts(v), axis=0)
        return rows_sum(add_parts(nn(left, ohl[...])) * one(high == row_high))

    arrive = [arrivals(0), arrivals(1)]
    inject(0)
    inject(1)

    def um_copy(t, j):
        return copy(um.at[t, d], um.at[t, d], um_s.at[t], um_r.at[t, d], n, dev(j))

    def um_wait(t, j):
        return copy(um.at[t, dev(j)], um.at[t, dev(j)], um_s.at[t], um_r.at[t, dev(j)], n, dev(j))

    def um_all(t):
        sent = um.at[t, pl.ds(0, DEVS - 1)]
        return copy(sent, sent, um_s.at[t], um_r.at[t, d], n, dev(1))

    def vv_copy(half, j, sender):
        steps = pl.ds(0, STEPS - 2) if half == 0 else pl.ds(STEPS - 2, 2)
        return copy(vv.at[sender, steps], vv.at[sender, steps], vv_s.at[half, j], vv_r.at[half, sender], n, dev(j))

    def w_copy(t, way, j):
        return copy(wsend.at[t, way], wrecv.at[t, way, d], w_s.at[t], w_r.at[t], net(1 if way == 0 else NETS - 1), dev(j))

    def w_all(t):
        return copy(wrecv.at[t], wrecv.at[t], w_s.at[t], w_r.at[t], net(1), d)

    def send_waves(t):
        wave = mine * (sample(volts[t]) * twice - arrive[t])
        wsend[t, 0] = wave[:, :512]
        wsend[t, 1] = wave[:, 512:]
        for j in (2, 1, 3, 0):
            for way in range(2):
                w_copy(t, way, j).start()

    def take_waves(t):
        w_all(t).wait_recv()
        waves.append(jnp.concatenate([sum(wrecv[t, 1, j] for j in range(DEVS)),
                                      sum(wrecv[t, 0, j] for j in range(DEVS))], axis=1))
        arrive.append(arrivals(t + DMIN))
        inject(t + DMIN)

    def columns(t, c, s):
        tiles = um[t, c] + jl[t, c]
        total = None
        for e in range(2):
            lanes = pl.ds(pl.multiple_of(256 * c + 128 * e, 128), 128)
            term = z[s, :, lanes] * tiles[2 * s + e:2 * s + e + 1, :]
            total = term if total is None else total + term
        return total

    def solve(t):
        for s in range(4):
            acc[s] = columns(t, d, s)
        if t:
            um_wait(t, 1).wait_recv()
            um_wait(t, 3).wait_recv()
        for s in range(4):
            acc[s] = acc[s] + columns(t, dev(1), s) + columns(t, dev(3), s)
        if t:
            um_wait(t, 2).wait_recv()
        rows = []
        for s in range(4):
            total = acc[s] + columns(t, dev(2), s)
            rows.append(rows_sum(total[:128].T))
            rows.append(rows_sum(total[128:].T))
        return jnp.concatenate(rows, axis=0)

    def keep(t):
        for c in range(8):
            for s in range(4):
                spot = 1024 * s + 128 * c
                trace[t:t + 1, spot:spot + 128] = vv[c // 2, t, 2 * s + c % 2:2 * s + c % 2 + 1, :]

    def r_copy(b, k):
        return copy(rsend.at[b, k], rrecv.at[b, k], r_s.at[b], r_r.at[b], away(k, -1), d)

    def r_all(b):
        rest = pl.ds(1, NETS - 1)
        return copy(rsend.at[b, rest], rrecv.at[b, rest], r_s.at[b], r_r.at[b], away(1), d)

    def send_back(b, steps):
        full = jnp.concatenate([vv[c, t] for t in steps for c in range(DEVS)], axis=0)
        reached = sum(nn(piece, hots[0]) for piece in parts(full))
        pick = one(slot_high[0] == high32)
        seats = one(iota((CAP, 512), 1) % CAP == iota((CAP, 512), 0))
        home = one(iota((NETS, 512), 1) // CAP == iota((NETS, 512), 0)).astype(BF16)
        table = [rows_sum(reached[32 * i:32 * i + 32] * pick) * seats for i in range(len(steps))]
        table.append(jnp.zeros((128 - CAP * len(steps), 512), F32))
        back = sum(nt(home, piece) for piece in parts(jnp.concatenate(table, axis=0)))
        rsend[b, :, 0, :] = back
        rrecv[b, 0] = back[0:1, :]
        for k in FAR_FIRST:
            r_copy(b, k).start()

    def last_copy(g):
        return copy(lsend.at[g // NETS, g % NETS // 8], lrecv.at[g], e_s, e_r, away(g % NETS, -1), dev(g // NETS))

    def last_all():
        rest = pl.ds(1, NETS * DEVS - 1)
        return copy(lrecv.at[rest], lrecv.at[rest], e_s, e_r, away(1), d)

    def pick_last(i, v):
        left = jnp.concatenate(parts(v), axis=0)
        for j in range(DEVS):
            line = rows_sum(add_parts(nn(left, hots[j])) * brow[j])
            for g in range(4):
                lsend[j, g, i:i + 1, :] = line[:, 128 * g:128 * g + 128]

    def send_last():
        lrecv[0] = lsend[0, 0]
        for g in ALL_FAR_FIRST[:30]:
            last_copy(g).start()
        for j in (2, 1, 3):
            vv_copy(1, j, d).start()
        for g in ALL_FAR_FIRST[30:]:
            last_copy(g).start()

    free, gain, volts = [], [], []
    passes(2, b=1, r=1)
    first_all().wait_recv()
    got = place_batch(0, 7)
    free += got[:4]
    gain += got[4:]
    for load in loads[11:]:
        load.wait()
    for c in range(DEVS):
        um[0, c] = jnp.concatenate([src[s, c] for s in range(4)], axis=0) + free[0][8 * c:8 * c + 8]
    base = jnp.concatenate([src[s, d] for s in range(4)], axis=0)
    for t in range(STEPS):
        if 1 <= t <= STEPS - DMIN:
            send_waves(t - 1)
        if t == 1:
            send_batch(1, [free_of(2, 2), gain_of(1, 2), gain_of(2, 2)])
            passes(3, x=2, b=2, r=2)
            passes(4, x=3)
        if t == 2:
            send_batch(2, [free_of(3, 2), free_of(3, 3), free_of(4, 3), gain_of(3, 2), gain_of(3, 3)])
        if t >= 2:
            take_waves(t - 2)
        if t == 2:
            share_batch(1)
        if t == 3:
            got = place_batch(1, 3)
            free += got[:1]
            gain += got[1:]
            passes(5, x=4)
            share_batch(2)
        if t == 4:
            passes(6, x=5)
            got = place_batch(2, 5)
            free += got[:3]
            gain += got[3:]
        if t == 5:
            passes(7, x=6, b=3)
        if t == 6:
            for j in (2, 1, 3):
                vv_copy(0, j, d).start()
            passes(8, x=7, b=4)
        if t == 7:
            for j in range(1, DEVS):
                vv_copy(0, j, dev(j)).wait_recv()
            send_back(0, list(range(STEPS - 2)))
            pick_last(0, volts[-1])
        ready = base
        if t + 1 < STEPS:
            ready = ready + free[t + 1]
            for k in range(t):
                ready = ready + gain[t - k] * volts[k]
        v = solve(t)
        volts.append(v)
        if t + 1 < STEPS:
            um[t + 1, d] = ready + gain[0] * v
            for j in (2, 1, 3):
                um_copy(t + 1, j).start()
        vv[d, t] = v
    pick_last(1, volts[-1])
    send_last()

    passes(9, b=5)
    passes(10, b=6)
    for t in range(STEPS - 2):
        keep(t)
    line_copy.wait_send()
    first_all().wait_send()
    for b in range(1, 3):
        a_all(b).wait_send()
        for j in range(1, DEVS):
            v_copy(b, j).wait_send()
    for t in range(1, STEPS):
        um_all(t).wait_send()
    for j in range(1, DEVS):
        vv_copy(0, j, d).wait_send()
        vv_copy(1, j, d).wait_send()
    for t in range(STEPS - DMIN):
        w_all(t).wait_send()
    r_all(0).wait_recv()
    by_seat = sum(tn(piece, own) for piece in parts(rrecv[0, :, 0, :]))
    state = xp[8]
    for t in range(STEPS - 2):
        state = state + rows_sum(by_seat[CAP * t:CAP * t + CAP] * seat) * xb[STEPS - 1 - t]
    state = state.T
    next_gain = xb[1].T
    spot = CAP * (offset - 8.0 * jnp.floor(offset * 0.125)) + rank
    spots = one(iota_f((128, 128), 0) == spot).T
    r_all(0).wait_send()
    for j in range(1, DEVS):
        vv_copy(1, j, dev(j)).wait_recv()
    keep(STEPS - 2)
    keep(STEPS - 1)
    last_all().wait_recv()
    columns_of = []
    for i in range(2):
        answer = sum(lrecv[NETS * j:NETS * j + NETS, i, :] for j in range(DEVS))
        by_model = sum(tn(own, piece) for piece in parts(answer))
        columns_of.append(jnp.sum(by_model * spots, axis=1, keepdims=True))
    final[...] = state + columns_of[0] * next_gain + columns_of[1] * gi[...]
    last_all().wait_send()


def hand_out(trace, final, trace_out, final_out, sems):
    copies = [pltpu.make_async_copy(trace, trace_out, sems.at[0]), pltpu.make_async_copy(final, final_out, sems.at[1])]
    for one_copy in copies:
        one_copy.start()
    for one_copy in copies:
        one_copy.wait()


def body(zinv, source, model_state, propagator, input_gain, output_gain, model_owner, model_bus,
         line_from, line_to, line_delay, line_imped, wave_from_past, wave_to_past):
    vmem, dma = pltpu.VMEM, pltpu.SemaphoreType.DMA
    i32 = jnp.int32
    scratch = [
        vmem((4, 256, 1024), F32), vmem((4, DEVS, 2, 128), F32), vmem((128, 128), F32), vmem((128, 128), F32),
        vmem((128, 128), F32), vmem((1, 128), i32), vmem((1, 128), i32), vmem((1, 512), i32), vmem((1, 512), i32),
        vmem((1, 512), i32), vmem((1, 512), F32), vmem((DMAX, 512), F32), vmem((DMAX, 512), F32),
        vmem((16, 128, 8, 128), F32), vmem((128, 128, 128), F32), vmem((STEPS + 1, 128, 128), F32),
        vmem((STEPS, 128, 128), F32), vmem((4, 128, 128), F32), vmem((3, NETS, 1, 128), F32),
        vmem((3, NETS, 1, 128), F32), vmem((NETS * DEVS, 1, 128), F32), vmem((3, DEVS, 8, 512), F32), vmem((STEPS, DEVS, 8, 128), F32), vmem((DEVS, STEPS, 8, 128), F32), vmem((16, 512), F32),
        vmem((16, 512), F32), vmem((6, 2, 1, 512), F32), vmem((6, 2, DEVS, 1, 512), F32),
        vmem((1, NETS, 1, 128), F32), vmem((1, NETS, 1, 128), F32),
        vmem((DEVS, 4, 2, 128), F32), vmem((NETS * DEVS, 2, 128), F32), vmem((128, 1024), BF16),
        vmem((DEVS, 128, 512), BF16), vmem((DEVS, 8, 512), F32), vmem((4, 256, 128), F32),
        vmem((STEPS, DEVS, 8, 128), F32),
        dma((13,)), dma((16,)), dma((3,)), dma((3,)), dma((3, DEVS)), dma((3, DEVS)),
        dma((STEPS,)), dma((STEPS, DEVS)), dma((2, DEVS)), dma((2, DEVS)), dma((6,)), dma((6,)), dma, dma, dma((1,)), dma((1,)), dma, dma,
    ]
    v = pl.BlockSpec(memory_space=vmem)
    found = pl.pallas_call(
        grid_kernel,
        out_shape=(vmem((STEPS, 4096), F32), vmem((128, 128), F32)),
        in_specs=[pl.BlockSpec(memory_space=pl.ANY)] * 14,
        out_specs=(v, v),
        scratch_shapes=scratch,
        compiler_params=pltpu.CompilerParams(collective_id=0, has_side_effects=True, vmem_limit_bytes=56 << 20),
    )(zinv, source.reshape(4, DEVS, 2, 128), model_state, propagator, input_gain, output_gain,
      model_owner.reshape(1, 128), model_bus.reshape(1, 128), line_from.reshape(1, 512), line_to.reshape(1, 512),
      line_delay.reshape(1, 512), line_imped.reshape(1, 512), wave_from_past, wave_to_past)
    return pl.pallas_call(
        hand_out,
        out_shape=(jax.ShapeDtypeStruct((STEPS, 4096), F32), jax.ShapeDtypeStruct((128, 128), F32)),
        in_specs=[v, v],
        out_specs=(pl.BlockSpec(memory_space=pl.ANY), pl.BlockSpec(memory_space=pl.ANY)),
        scratch_shapes=[dma((2,))],
        compiler_params=pltpu.CompilerParams(vmem_limit_bytes=40 << 20),
    )(*found)


def solution(mesh):
    one_axis, both = P("net"), P(("net", "dev"))
    two = P(("net", "dev"), None)
    in_specs = (P("net", "dev", None), one_axis, two, P(("net", "dev"), None, None), two, two, two, both,
                one_axis, one_axis, one_axis, one_axis, P(None, "net"), P(None, "net"))
    return jax.shard_map(body, mesh=mesh, in_specs=in_specs, out_specs=(P(None, "net"), two), check_vma=False)
```
